32 devices in a mesh: ctx: 8 (over y, x, core), tp: 4 (over z).
Axes of the slice: x: 2, y: 2, z: 4, core: 2. Of those that a mesh axis runs over, the one named last changes fastest.
Arguments:
- queries: bfloat16 [2, 8, 128, 8192], P(None, 'ctx', None, 'tp'), may hold values from -5 to 5
- keys: bfloat16 [2, 8, 128, 1024], P(None, 'ctx', None, 'tp'), may hold values from -5 to 5
- values: bfloat16 [2, 8, 128, 1024], P(None, 'ctx', None, 'tp'), may hold values from -6 to 6
- out_grad: bfloat16 [2, 8, 128, 8192], P(None, 'ctx', None, 'tp'), may hold values from -6 to 6
- block_doc: int32 [16], replicated, may hold values from 0 to 15, as said below
Outputs:
- attn_out: bfloat16 [2, 8, 128, 8192], P(None, 'ctx', None, 'tp')
- query_grad: bfloat16 [2, 8, 128, 8192], P(None, 'ctx', None, 'tp')
- key_grad: bfloat16 [2, 8, 128, 1024], P(None, 'ctx', None, 'tp')
- value_grad: bfloat16 [2, 8, 128, 1024], P(None, 'ctx', None, 'tp')
The draws below stay inside these ranges and needn't reach their ends.
Inputs may be any that keep to these rules, and one draw needn't show every extreme that they name: block_doc never falls along the sequence; each document covers 1 to 2 consecutive blocks, and in each half of the sequence the first document covers exactly 2; no document holds both block 7 and block 8; the first block's id is 0 and the last block's id is 15.
All inputs are finite; a program needn't handle non-finite values.
Results may differ from the reference program's by a relative error of at most 0.0094.
Values may be sent and summed in bfloat16 or wider, within the bound.
No kernel may reach another device: no remote copies, remote signals or barrier semaphores. Data moves between devices by JAX's collectives and lax.ppermute only.
A program may use at most 64 MiB of HBM per device.

```python
import math
import jax
import jax.numpy as jnp
from jax import lax

HQ = 64
HK = 8
HD = 128
BLOCK = 128
PIECE = 128
GROUP = 8
SEQ = 2048
NBLK = 16
MAXB = 2
N_CTX = 8


def draw_queries(key, part):
    pair_count = SEQ // (2 * PIECE)
    full_shape = (2, pair_count, PIECE, HQ * HD)
    return jnp.clip(jax.random.normal(jax.random.fold_in(key, 11), full_shape, jnp.float32), -5.0, 5.0).astype(jnp.bfloat16)


def draw_keys(key, part):
    pair_count = SEQ // (2 * PIECE)
    full_shape = (2, pair_count, PIECE, HK * HD)
    return jnp.clip(jax.random.normal(jax.random.fold_in(key, 31), full_shape, jnp.float32), -5.0, 5.0).astype(jnp.bfloat16)


def draw_block_doc(key, part):
    half_blocks = NBLK // 2

    def one_half(sub_key):
        lengths = jax.random.randint(sub_key, (half_blocks,), 1, MAXB + 1)
        lengths = jnp.where(jnp.arange(half_blocks) == 0, MAXB, lengths)
        starts = jnp.cumsum(lengths) - lengths
        blocks = jnp.arange(half_blocks)
        return jnp.sum((starts[None, :] <= blocks[:, None]).astype(jnp.int32), axis=1) - 1
    first_half = one_half(jax.random.fold_in(key, 21))
    second_local = one_half(jax.random.fold_in(key, 22))
    second_count = second_local[half_blocks - 1] + 1
    second_half = second_local + (NBLK - second_count)
    return jnp.concatenate([first_half, second_half]).astype(jnp.int32)


def block_levels(own_key, dims, pieces, least, largest):
    level = 1.0
    for position, shards_of in pieces:
        draws = jax.random.uniform(jax.random.fold_in(jax.random.fold_in(own_key, 6), position), (shards_of,), jnp.float32, least / len(pieces), largest / len(pieces))
        level = level * jnp.repeat(jnp.exp(draws), dims[position] // shards_of).reshape((-1,) + (1,) * (len(dims) - 1 - position))
    return level


def noise(key, dims, scale, most, split=(), kind=jnp.bfloat16):
    loudness = block_levels(key, dims, split, -0.22, 0.18) if split else 1.0
    array = jax.random.normal(key, dims, jnp.float32) * scale * loudness
    return jnp.minimum(jnp.maximum(array, -most), most).astype(kind)


def setup_inputs(seed: int = 0) -> dict:
    seeds = jax.random.split(jax.random.key(seed), 6)
    queries = draw_queries(jax.random.fold_in(seeds[5], 71), 0)
    keys = draw_keys(jax.random.fold_in(seeds[5], 71), 0)
    values = noise(seeds[2], (2, N_CTX, PIECE, HK * HD), 1.0, 6.0, ((1, 8), (3, 4)))
    out_grad = noise(seeds[3], (2, N_CTX, PIECE, HQ * HD), 1.0, 6.0, ((1, 8), (3, 4)))
    block_doc = draw_block_doc(jax.random.fold_in(seeds[5], 71), 0)
    return dict(queries=queries, keys=keys, values=values, out_grad=out_grad, block_doc=block_doc)


masked_score = -1e+30

def to_sequence(arranged):
    return jnp.concatenate([arranged[0], arranged[1][::-1]], axis=0)

def to_pairs(ordered, pair_count):
    return jnp.stack([ordered[:pair_count], ordered[pair_count:][::-1]])

def reference(queries, keys, values, out_grad, block_doc):
    pair_count = queries.shape[1]
    scaling = 1.0 / math.sqrt(HD)
    padding = MAXB - 1
    query_seq = to_sequence(queries).reshape(NBLK, BLOCK, HK, GROUP, HD)
    grad_seq = to_sequence(out_grad).reshape(NBLK, BLOCK, HK, GROUP, HD)
    key_seq = to_sequence(keys).reshape(NBLK, BLOCK, HK, HD)
    value_seq = to_sequence(values).reshape(NBLK, BLOCK, HK, HD)
    key_pad = jnp.concatenate([jnp.zeros((padding, BLOCK, HK, HD), key_seq.dtype), key_seq], axis=0)
    value_pad = jnp.concatenate([jnp.zeros((padding, BLOCK, HK, HD), value_seq.dtype), value_seq], axis=0)
    doc_pad = jnp.concatenate([jnp.full((padding,), -1, jnp.int32), block_doc.astype(jnp.int32)])
    offsets = jnp.arange(BLOCK, dtype=jnp.int32)
    window_offsets = jnp.arange(MAXB * BLOCK, dtype=jnp.int32)

    def visit(carry, block_index):
        key_acc, value_acc = carry
        query_block = lax.dynamic_index_in_dim(query_seq, block_index, 0, keepdims=False).astype(jnp.float32)
        grad_block = lax.dynamic_index_in_dim(grad_seq, block_index, 0, keepdims=False).astype(jnp.float32)
        key_window = lax.dynamic_slice_in_dim(key_pad, block_index, MAXB, 0).reshape(MAXB * BLOCK, HK, HD).astype(jnp.float32)
        value_window = lax.dynamic_slice_in_dim(value_pad, block_index, MAXB, 0).reshape(MAXB * BLOCK, HK, HD).astype(jnp.float32)
        key_docs = jnp.repeat(lax.dynamic_slice_in_dim(doc_pad, block_index, MAXB, 0), BLOCK)
        query_doc = lax.dynamic_index_in_dim(block_doc.astype(jnp.int32), block_index, 0, keepdims=False)
        query_pos = block_index * BLOCK + offsets
        key_pos = (block_index - padding) * BLOCK + window_offsets
        visible = (key_docs[None, :] == query_doc) & (key_pos[None, :] <= query_pos[:, None])
        scores = jnp.einsum('qhgd,khd->hgqk', query_block, key_window) * scaling
        scores = jnp.where(visible, scores, masked_score)
        row_max = lax.optimization_barrier(jnp.max(scores, axis=-1, keepdims=True))
        log_total = row_max + jnp.log(lax.optimization_barrier(jnp.sum(jnp.exp(scores - row_max), axis=-1, keepdims=True)))
        probs = jnp.exp(scores - log_total)
        probs_low = lax.optimization_barrier(probs.astype(jnp.bfloat16)).astype(jnp.float32)
        attended = jnp.einsum('hgqk,khd->qhgd', probs_low, value_window)
        out_low = attended.astype(jnp.bfloat16)
        out_back = lax.optimization_barrier(out_low).astype(jnp.float32)
        delta = jnp.einsum('qhgd,qhgd->hgq', grad_block, out_back)
        dprobs = jnp.einsum('qhgd,khd->hgqk', grad_block, value_window)
        dscores = lax.optimization_barrier((probs * (dprobs - delta[..., None])).astype(jnp.bfloat16)).astype(jnp.float32)
        query_part = jnp.einsum('hgqk,khd->qhgd', dscores, key_window) * scaling
        key_part = (jnp.einsum('hgqk,qhgd->khd', dscores, query_block) * scaling).reshape(MAXB, BLOCK, HK, HD)
        value_part = jnp.einsum('hgqk,qhgd->khd', probs_low, grad_block).reshape(MAXB, BLOCK, HK, HD)
        key_acc = lax.dynamic_update_slice_in_dim(key_acc, lax.dynamic_slice_in_dim(key_acc, block_index, MAXB, 0) + key_part, block_index, 0)
        value_acc = lax.dynamic_update_slice_in_dim(value_acc, lax.dynamic_slice_in_dim(value_acc, block_index, MAXB, 0) + value_part, block_index, 0)
        return ((key_acc, value_acc), (out_low, query_part.astype(jnp.bfloat16)))
    zero_acc = jnp.zeros((NBLK + padding, BLOCK, HK, HD), jnp.float32)
    (key_acc, value_acc), (outs_all, qgrads_all) = lax.scan(visit, (zero_acc, zero_acc), jnp.arange(NBLK, dtype=jnp.int32))
    attn_out = to_pairs(outs_all.reshape(2 * pair_count, PIECE, HQ * HD), pair_count)
    query_grad = to_pairs(qgrads_all.reshape(2 * pair_count, PIECE, HQ * HD), pair_count)
    key_grad = to_pairs(key_acc[padding:].astype(jnp.bfloat16).reshape(2 * pair_count, PIECE, HK * HD), pair_count)
    value_grad = to_pairs(value_acc[padding:].astype(jnp.bfloat16).reshape(2 * pair_count, PIECE, HK * HD), pair_count)
    return (attn_out, query_grad, key_grad, value_grad)
```

```python
import math

import jax
import jax.numpy as jnp
from jax import lax
from jax.experimental import pallas as pl
from jax.experimental.pallas import tpu as pltpu
from jax.sharding import PartitionSpec as P

HQ = 64
HK = 8
HD = 128
BLOCK = 128


masked_score = -1e30


def shifted(block, axis, distance):
    devices = range(lax.axis_size(axis))
    route = [(i - distance, i) for i in devices if i - distance in devices]
    return lax.ppermute(block, axis, route)


def move_keys(payload, distance):
    return shifted(payload, "ctx", distance)


def move_grads(payload, distance):
    return shifted(payload.astype(jnp.bfloat16), "ctx", distance).astype(payload.dtype)


def piece_docs(block_doc, piece_index, piece_len):
    per_piece = piece_len // BLOCK
    start = jnp.maximum(piece_index, 0) * per_piece
    doc_blocks = lax.dynamic_slice_in_dim(block_doc, start, per_piece, 0)
    doc_tokens = jnp.repeat(doc_blocks, BLOCK)
    return jnp.where(piece_index >= 0, doc_tokens, -1)


def attend(query_piece, grad_piece, key_buffer, piece_index, block_doc):
    window, _, piece_len, features = key_buffer.shape
    kv_heads = features // HD
    scaling = 1.0 / math.sqrt(HD)
    key_slots = key_buffer[:, 0].reshape(window, piece_len, kv_heads, HD)
    value_slots = key_buffer[:, 1].reshape(window, piece_len, kv_heads, HD)
    keys_flat = key_slots.reshape(window * piece_len, kv_heads, HD)
    values_flat = value_slots.reshape(window * piece_len, kv_heads, HD)
    positions = jnp.arange(piece_len, dtype=jnp.int32)
    query_docs = piece_docs(block_doc, piece_index, piece_len)
    query_pos = piece_index * piece_len + positions
    visible_rows = []
    for slot_index in range(window):
        key_index = piece_index - (window - 1) + slot_index
        key_docs = piece_docs(block_doc, key_index, piece_len)
        key_pos = key_index * piece_len + positions
        visible_rows.append(
            (key_docs[None, :] == query_docs[:, None]) & (key_pos[None, :] <= query_pos[:, None])
        )
    visible = jnp.concatenate(visible_rows, axis=1)

    def key_side(form, left, flat):
        return jnp.einsum(form, left, flat, preferred_element_type=jnp.float32)

    def key_sum(form, weights, flat):
        return jnp.einsum(form, weights, flat, preferred_element_type=jnp.float32)

    def per_key(form, weights, right):
        return jnp.einsum(form, weights, right, preferred_element_type=jnp.float32).reshape(
            window, piece_len, kv_heads, HD
        )

    raw_scores = key_side("qhgd,khd->hgqk", query_piece, keys_flat)
    scores = jnp.where(visible[None, None], raw_scores * scaling, masked_score)
    row_max = jnp.max(scores, axis=-1, keepdims=True)
    log_total = row_max + jnp.log(jnp.sum(jnp.exp(scores - row_max), axis=-1, keepdims=True))
    probs = jnp.exp(scores - log_total)
    probs_low = probs.astype(jnp.bfloat16)
    attended = key_sum("hgqk,khd->qhgd", probs_low, values_flat)
    out_low = attended.astype(jnp.bfloat16)
    out_back = lax.optimization_barrier(out_low).astype(jnp.float32)
    delta = jnp.einsum("qhgd,qhgd->hgq", grad_piece.astype(jnp.float32), out_back)
    dprobs = key_side("qhgd,khd->hgqk", grad_piece, values_flat)
    dscores = (probs * (dprobs - delta[..., None])).astype(jnp.bfloat16)
    query_part = (key_sum("hgqk,khd->qhgd", dscores, keys_flat) * scaling).astype(jnp.bfloat16)
    key_part = per_key("hgqk,qhgd->khd", dscores, query_piece) * scaling
    value_part = per_key("hgqk,qhgd->khd", probs_low, grad_piece)
    grads = jnp.stack(
        [
            key_part.reshape(window, piece_len, features),
            value_part.reshape(window, piece_len, features),
        ],
        axis=1,
    )
    return (out_low.reshape(piece_len, -1), query_part.reshape(piece_len, -1), grads)


def local_wide(queries, keys, values, out_grad, block_doc):
    ctx_size = lax.axis_size("ctx")
    my_index = lax.axis_index("ctx")
    reach_back = min(7, ctx_size // 4 - 1)
    window = reach_back + 1
    levels = window.bit_length() - 1
    piece_len = queries.shape[2]
    kv_heads = keys.shape[3] // HD
    group = HQ // HK
    query_all = queries[:, 0].reshape(2, piece_len, kv_heads, group, HD)
    grad_all = out_grad[:, 0].reshape(2, piece_len, kv_heads, group, HD)
    paired = jnp.stack([keys[:, 0], values[:, 0]], axis=1)
    low_buffer = paired[0][None]
    high_buffer = paired[1][None]
    for level_bit in range(levels):
        distance = 1 << level_bit
        low_buffer = jnp.concatenate([move_keys(low_buffer, distance), low_buffer], axis=0)
        high_buffer = jnp.concatenate([move_keys(high_buffer, -distance), high_buffer], axis=0)
    high_index = 2 * ctx_size - 1 - my_index
    low_out, low_qgrad, low_grads = attend(
        query_all[0], grad_all[0], low_buffer, my_index, block_doc
    )
    high_out, high_qgrad, high_grads = attend(
        query_all[1], grad_all[1], high_buffer, high_index, block_doc
    )
    low_back = low_grads
    high_back = high_grads
    for level_bit in reversed(range(levels)):
        distance = 1 << level_bit
        low_back = low_back[distance:] + move_grads(low_back[:distance], -distance)
        high_back = high_back[distance:] + move_grads(high_back[:distance], distance)
    low_total = low_back[0]
    high_total = high_back[0]
    attn_pair = jnp.stack([low_out, high_out])[:, None]
    qgrad_pair = jnp.stack([low_qgrad, high_qgrad])[:, None]
    key_pair = jnp.stack([low_total[0], high_total[0]]).astype(jnp.bfloat16)[:, None]
    value_pair = jnp.stack([low_total[1], high_total[1]]).astype(jnp.bfloat16)[:, None]
    return (attn_pair, qgrad_pair, key_pair, value_pair)


GROUP = HQ // HK
CHUNK = 2 * HD
LOG2_SCALE = math.log2(math.e) / math.sqrt(HD)
SCALE = 1.0 / math.sqrt(HD)
VMEM_LIMIT = 24 * 1024 * 1024

F32 = jnp.float32
BF16 = jnp.bfloat16

in_vmem = pl.BlockSpec(memory_space=pltpu.VMEM)
in_hbm = pl.BlockSpec(memory_space=pltpu.HBM)
in_smem = pl.BlockSpec(memory_space=pltpu.SMEM)


def dot(left, right):
    return jnp.dot(left, right, preferred_element_type=F32)


def dot_t(left, right):
    return lax.dot_general(left, right, (((1,), (1,)), ((), ())), preferred_element_type=F32)


def near_slot():
    return lax.rem(lax.axis_index("ctx"), 2)


def far_slot():
    return 1 - near_slot()


def linked(doc_ref, slot):
    pairs = lax.axis_size("ctx")
    me = lax.axis_index("ctx")
    piece = jnp.where(slot == 0, me, 2 * pairs - 1 - me)
    same = doc_ref[piece] == doc_ref[jnp.maximum(piece - 1, 0)]
    return jnp.where(jnp.logical_and(piece > 0, same), 0.0, masked_score).astype(F32)


def lanes(ref, first, count):
    parts = [ref[:, pl.ds(first + i * HD, HD)] for i in range(count)]
    return jnp.concatenate(parts, axis=0)


def causal(rows, columns):
    key = lax.broadcasted_iota(jnp.int32, (rows, columns), 0)
    query = lax.broadcasted_iota(jnp.int32, (rows, columns), 1)
    return key <= lax.rem(query, rows)


def fetch_pairs(pairs_of_refs, sems):
    copies = [pltpu.make_async_copy(a, b, sems.at[i]) for i, (a, b) in enumerate(pairs_of_refs)]
    for copy in copies:
        copy.start()
    return copies


def pick_kernel(keys, values, far_kv, near_kv, sems):
    far, near = far_slot(), near_slot()
    copies = fetch_pairs(
        [
            (keys.at[far, 0], far_kv.at[0]),
            (values.at[far, 0], far_kv.at[1]),
            (keys.at[near, 0], near_kv.at[0]),
            (values.at[near, 0], near_kv.at[1]),
        ],
        sems,
    )
    for copy in copies:
        copy.wait()


def pick(keys, values):
    _, _, piece_len, features = keys.shape
    shape = pltpu.VMEM((2, piece_len, features), BF16)
    return pl.pallas_call(
        pick_kernel,
        out_shape=(shape, shape),
        in_specs=[in_hbm, in_hbm],
        out_specs=(in_vmem, in_vmem),
        scratch_shapes=[pltpu.SemaphoreType.DMA((4,))],
        name="pick",
    )(keys, values)


def keep_kernel(*refs):
    pass


def keep(far_kv, near_kv):
    shape = pltpu.VMEM(far_kv.shape, BF16)
    return pl.pallas_call(
        keep_kernel,
        out_shape=(shape, shape),
        in_specs=[in_vmem, in_vmem],
        out_specs=(in_vmem, in_vmem),
        input_output_aliases={0: 0, 1: 1},
        cost_estimate=pl.CostEstimate(flops=10**10, bytes_accessed=10**6, transcendentals=0),
        compiler_params=pltpu.CompilerParams(vmem_limit_bytes=VMEM_LIMIT),
        name="keep",
    )(far_kv, near_kv)


def diagonal_kernel(doc, kv, queries, out_grad, weights, dprobs, stats):
    near = near_slot()
    q, do = queries.at[near, 0], out_grad.at[near, 0]
    kv_heads = kv.shape[2] // HD
    bias = linked(doc, near)
    mask = causal(kv.shape[1], CHUNK)
    for j in range(kv_heads):
        k = kv[0, :, pl.ds(j * HD, HD)]
        v = kv[1, :, pl.ds(j * HD, HD)]
        for h in range(0, GROUP, 2):
            first = (j * GROUP + h) * HD
            at = pl.ds(first, CHUNK)
            logits = jnp.where(mask, dot_t(k, lanes(q, first, 2)) * LOG2_SCALE, masked_score)
            top = jnp.max(logits, axis=0, keepdims=True)
            e = jnp.exp2(logits - top)
            dp = dot_t(v, lanes(do, first, 2))
            weights[:, at] = e
            dprobs[:, at] = dp
            stats[0:1, at] = top
            stats[1:2, at] = jnp.sum(e, axis=0, keepdims=True)
            stats[2:3, at] = jnp.sum(e * dp, axis=0, keepdims=True)
            stats[3:4, at] = jnp.full((1, CHUNK), bias, F32)


def diagonal(block_doc, kv, queries, out_grad):
    _, _, piece_len, width = queries.shape
    return pl.pallas_call(
        diagonal_kernel,
        out_shape=(
            pltpu.VMEM((piece_len, width), F32),
            pltpu.VMEM((piece_len, width), F32),
            pltpu.VMEM((8, width), F32),
        ),
        in_specs=[in_smem, in_vmem, in_vmem, in_vmem],
        out_specs=(in_vmem,) * 3,
        compiler_params=pltpu.CompilerParams(vmem_limit_bytes=VMEM_LIMIT),
        name="diagonal",
    )(block_doc, kv, queries, out_grad)


def whole_kernel(doc, kv, kv_before, queries, out_grad, before, own, p, ds):
    far = far_slot()
    q, do = queries.at[far, 0], out_grad.at[far, 0]
    kv_heads = kv.shape[2] // HD
    piece_len = kv.shape[1]
    bias = linked(doc, far)
    mask = causal(piece_len, CHUNK)
    for j in range(kv_heads):
        head = pl.ds(j * HD, HD)
        k = jnp.concatenate([kv_before[0, :, head], kv[0, :, head]], axis=0)
        v = jnp.concatenate([kv_before[1, :, head], kv[1, :, head]], axis=0)
        for h in range(0, GROUP, 2):
            first = (j * GROUP + h) * HD
            at = pl.ds(first, CHUNK)
            logits = dot_t(k, lanes(q, first, 2)) * LOG2_SCALE
            cross = logits[:piece_len]
            here = jnp.where(mask, logits[piece_len:], masked_score)
            top = jnp.maximum(
                jnp.max(cross, axis=0, keepdims=True) + bias, jnp.max(here, axis=0, keepdims=True)
            )
            e = jnp.concatenate([jnp.exp2(cross - (top - bias)), jnp.exp2(here - top)], axis=0)
            dp = dot_t(v, lanes(do, first, 2))
            ratio = 1.0 / jnp.sum(e, axis=0, keepdims=True)
            delta = jnp.sum(e * dp, axis=0, keepdims=True) * ratio
            prob = e * ratio
            p[:, at] = prob.astype(BF16)
            ds[:, at] = (prob * (dp - delta)).astype(BF16)
        cols = pl.ds(j * GROUP * HD, GROUP * HD)
        dk = dot(ds[:, cols], lanes(q, j * GROUP * HD, GROUP)) * SCALE
        dv = dot(p[:, cols], lanes(do, j * GROUP * HD, GROUP))
        before[0, :, head] = dk[:piece_len].astype(BF16)
        before[1, :, head] = dv[:piece_len].astype(BF16)
        own[0, :, head] = dk[piece_len:]
        own[1, :, head] = dv[piece_len:]


def whole(block_doc, kv, kv_before, queries, out_grad):
    _, piece_len, features = kv.shape
    width = queries.shape[3]
    return pl.pallas_call(
        whole_kernel,
        out_shape=(
            pltpu.VMEM((2, piece_len, features), BF16),
            pltpu.VMEM((2, piece_len, features), F32),
            pltpu.VMEM((2 * piece_len, width), BF16),
            pltpu.VMEM((2 * piece_len, width), BF16),
        ),
        in_specs=[in_smem] + [in_vmem] * 4,
        out_specs=(in_vmem,) * 4,
        compiler_params=pltpu.CompilerParams(vmem_limit_bytes=VMEM_LIMIT),
        name="whole",
    )(block_doc, kv, kv_before, queries, out_grad)


def cross_kernel(kv_before, queries, out_grad, stats, before, p, ds, after):
    near = near_slot()
    q, do = queries.at[near, 0], out_grad.at[near, 0]
    piece_len, features = kv_before.shape[1:]
    for j in range(features // HD):
        head = pl.ds(j * HD, HD)
        k = kv_before[0, :, head]
        v = kv_before[1, :, head]
        for h in range(0, GROUP, 2):
            first = (j * GROUP + h) * HD
            at = pl.ds(first, CHUNK)
            top_here, total_here, dot_here, bias = (stats[i : i + 1, at] for i in range(4))
            logits = dot_t(k, lanes(q, first, 2)) * LOG2_SCALE
            top = jnp.maximum(jnp.max(logits, axis=0, keepdims=True) + bias, top_here)
            e = jnp.exp2(logits - (top - bias))
            dp = dot_t(v, lanes(do, first, 2))
            shrink = jnp.exp2(top_here - top)
            ratio = 1.0 / (total_here * shrink + jnp.sum(e, axis=0, keepdims=True))
            delta = (dot_here * shrink + jnp.sum(e * dp, axis=0, keepdims=True)) * ratio
            prob = e * ratio
            p[:, at] = prob.astype(BF16)
            ds[:, at] = (prob * (dp - delta)).astype(BF16)
            after[0:1, at] = shrink * ratio
            after[1:2, at] = delta
        cols = pl.ds(j * GROUP * HD, GROUP * HD)
        dk = dot(ds[:, cols], lanes(q, j * GROUP * HD, GROUP)) * SCALE
        dv = dot(p[:, cols], lanes(do, j * GROUP * HD, GROUP))
        before[0, :, head] = dk.astype(BF16)
        before[1, :, head] = dv.astype(BF16)


def cross(kv_before, queries, out_grad, stats):
    _, piece_len, features = kv_before.shape
    width = queries.shape[3]
    return pl.pallas_call(
        cross_kernel,
        out_shape=(
            pltpu.VMEM((2, piece_len, features), BF16),
            pltpu.VMEM((piece_len, width), BF16),
            pltpu.VMEM((piece_len, width), BF16),
            pltpu.VMEM((8, width), F32),
        ),
        in_specs=[in_vmem] * 4,
        out_specs=(in_vmem,) * 4,
        compiler_params=pltpu.CompilerParams(vmem_limit_bytes=VMEM_LIMIT),
        name="cross",
    )(kv_before, queries, out_grad, stats)


def turn(wide, ref, first):
    for i in range(wide.shape[1] // HD):
        ref[:, pl.ds(first + i * HD, HD)] = wide[:, i * HD : (i + 1) * HD].T


def rest_kernel(
    near_kv, next_kv, queries, out_grad, weights, dprobs, p_next, ds_next, after, passed, far_kv, mate_kv,
    p_far, ds_far, out, q_grad, k_grad, v_grad, o, dq, p, ds, dk_low, dv_low, sems,
):
    near, far = near_slot(), far_slot()
    q, do = queries.at[near, 0], out_grad.at[near, 0]
    kv_heads = near_kv.shape[2] // HD
    span = GROUP * HD
    backs = []

    def give_back(side, slot, j):
        cols = pl.ds(j * span, span)
        for n, (a, b) in enumerate(((o, out), (dq, q_grad))):
            sem = sems.at[2 + (side * kv_heads + j) * 2 + n]
            back = pltpu.make_async_copy(a.at[side, :, cols], b.at[slot, 0, :, cols], sem)
            back.start()
            backs.append(back)

    for j in range(kv_heads):
        head = pl.ds(j * HD, HD)
        k_t = jnp.concatenate([mate_kv[0, :, head], far_kv[0, :, head]], axis=0).T
        v_t = jnp.concatenate([mate_kv[1, :, head], far_kv[1, :, head]], axis=0).T
        for h in range(0, GROUP, 2):
            first = (j * GROUP + h) * HD
            at = pl.ds(first, CHUNK)
            turn(dot(v_t, p_far[:, at]).astype(BF16), o.at[1], first)
            turn((dot(k_t, ds_far[:, at]) * SCALE).astype(BF16), dq.at[1], first)
        give_back(1, far, j)
    for j in range(kv_heads):
        head = pl.ds(j * HD, HD)
        k_t = jnp.concatenate([next_kv[0, :, head], near_kv[0, :, head]], axis=0).T
        v_t = jnp.concatenate([next_kv[1, :, head], near_kv[1, :, head]], axis=0).T
        for h in range(0, GROUP, 2):
            first = (j * GROUP + h) * HD
            at = pl.ds(first, CHUNK)
            prob = weights[:, at] * after[0:1, at]
            prob_low = prob.astype(BF16)
            ds_low = (prob * (dprobs[:, at] - after[1:2, at])).astype(BF16)
            p[:, pl.ds(h * HD, CHUNK)] = prob_low
            ds[:, pl.ds(h * HD, CHUNK)] = ds_low
            turn(dot(v_t, jnp.concatenate([p_next[:, at], prob_low], axis=0)).astype(BF16), o.at[0], first)
            dq_t = dot(k_t, jnp.concatenate([ds_next[:, at], ds_low], axis=0)) * SCALE
            turn(dq_t.astype(BF16), dq.at[0], first)
        give_back(0, near, j)
        dk = dot(ds[...], lanes(q, j * span, GROUP)) * SCALE
        dv = dot(p[...], lanes(do, j * span, GROUP))
        dk_low[:, head] = (dk + passed[0, :, head].astype(F32)).astype(BF16)
        dv_low[:, head] = (dv + passed[1, :, head].astype(F32)).astype(BF16)
    backs += fetch_pairs([(dk_low, k_grad.at[near, 0]), (dv_low, v_grad.at[near, 0])], sems)
    for back in backs:
        back.wait()


def rest(*operands, shape):
    _, piece_len, features = operands[0].shape
    width = shape[3]
    kv_heads = features // HD
    wide = jax.ShapeDtypeStruct(shape, BF16)
    small = jax.ShapeDtypeStruct(shape[:3] + (features,), BF16)
    return pl.pallas_call(
        rest_kernel,
        out_shape=(wide, wide, small, small),
        in_specs=[in_vmem] * len(operands),
        out_specs=(in_hbm,) * 4,
        scratch_shapes=[pltpu.VMEM((2, piece_len, width), BF16)] * 2
        + [pltpu.VMEM((piece_len, GROUP * HD), BF16)] * 2
        + [pltpu.VMEM((piece_len, features), BF16)] * 2
        + [pltpu.SemaphoreType.DMA((2 + 4 * kv_heads,))],
        compiler_params=pltpu.CompilerParams(vmem_limit_bytes=VMEM_LIMIT),
        name="rest",
    )(*operands)


def total_kernel(own, passed, k_grad_in, v_grad_in, k_grad, v_grad, low, sems):
    far = far_slot()
    low[...] = (own[...] + passed[...].astype(F32)).astype(BF16)
    copies = fetch_pairs([(low.at[0], k_grad.at[far, 0]), (low.at[1], v_grad.at[far, 0])], sems)
    for copy in copies:
        copy.wait()


def total(own, passed, k_grad, v_grad):
    return pl.pallas_call(
        total_kernel,
        out_shape=(jax.ShapeDtypeStruct(k_grad.shape, BF16),) * 2,
        in_specs=[in_vmem] * 2 + [in_hbm] * 2,
        out_specs=(in_hbm,) * 2,
        input_output_aliases={2: 0, 3: 1},
        scratch_shapes=[pltpu.VMEM(own.shape, BF16), pltpu.SemaphoreType.DMA((2,))],
        compiler_params=pltpu.CompilerParams(vmem_limit_bytes=VMEM_LIMIT),
        name="total",
    )(own, passed, k_grad, v_grad)


def local_pairs(queries, keys, values, out_grad, block_doc):
    pairs = lax.axis_size("ctx")
    mates = [(i, i ^ 1) for i in range(pairs) if i ^ 1 < pairs]
    low_route = [(i, i + 1) for i in range(3, pairs - 1, 2)]
    high_route = [(i + 1, i) for i in range(1, pairs - 3, 2)]
    route = low_route + high_route
    route_back = [(b, a) for a, b in route]
    far_kv, near_kv = keep(*pick(keys, values))
    mate_kv = lax.ppermute(near_kv, "ctx", mates)
    next_kv = lax.ppermute(far_kv, "ctx", route)
    weights, dprobs, stats = diagonal(block_doc, near_kv, queries, out_grad)
    mate_grads, own_grads, p_far, ds_far = whole(block_doc, far_kv, mate_kv, queries, out_grad)
    mate_back = lax.ppermute(mate_grads, "ctx", mates)
    next_grads, p_next, ds_next, after = cross(next_kv, queries, out_grad, stats)
    next_back = lax.ppermute(next_grads, "ctx", route_back)
    out, q_grad, k_grad, v_grad = rest(
        near_kv, next_kv, queries, out_grad, weights, dprobs, p_next, ds_next, after, mate_back,
        far_kv, mate_kv, p_far, ds_far, shape=queries.shape,
    )
    k_grad, v_grad = total(own_grads, next_back, k_grad, v_grad)
    return (out, q_grad, k_grad, v_grad)


def local(queries, keys, values, out_grad, block_doc):
    window = min(7, lax.axis_size("ctx") // 4 - 1) + 1
    piece_len = queries.shape[2]
    if window == 2 and piece_len == BLOCK:
        return local_pairs(queries, keys, values, out_grad, block_doc)
    return local_wide(queries, keys, values, out_grad, block_doc)


def solution(mesh):
    in_specs = (
        P(None, "ctx", None, "tp"),
        P(None, "ctx", None, "tp"),
        P(None, "ctx", None, "tp"),
        P(None, "ctx", None, "tp"),
        P(),
    )
    out_specs = (
        P(None, "ctx", None, "tp"),
        P(None, "ctx", None, "tp"),
        P(None, "ctx", None, "tp"),
        P(None, "ctx", None, "tp"),
    )
    return jax.shard_map(local, mesh=mesh, in_specs=in_specs, out_specs=out_specs, check_vma=False)
```

```python
import math

import jax
import jax.numpy as jnp
from jax import lax
from jax.experimental import pallas as pl
from jax.experimental.pallas import tpu as pltpu
from jax.sharding import PartitionSpec as P

HQ = 64
HK = 8
HD = 128
BLOCK = 128


masked_score = -1e30


def shifted(block, axis, distance):
    devices = range(lax.axis_size(axis))
    route = [(i - distance, i) for i in devices if i - distance in devices]
    return lax.ppermute(block, axis, route)


def move_keys(payload, distance):
    return shifted(payload, "ctx", distance)


def move_grads(payload, distance):
    return shifted(payload.astype(jnp.bfloat16), "ctx", distance).astype(payload.dtype)


def piece_docs(block_doc, piece_index, piece_len):
    per_piece = piece_len // BLOCK
    start = jnp.maximum(piece_index, 0) * per_piece
    doc_blocks = lax.dynamic_slice_in_dim(block_doc, start, per_piece, 0)
    doc_tokens = jnp.repeat(doc_blocks, BLOCK)
    return jnp.where(piece_index >= 0, doc_tokens, -1)


def attend(query_piece, grad_piece, key_buffer, piece_index, block_doc):
    window, _, piece_len, features = key_buffer.shape
    kv_heads = features // HD
    scaling = 1.0 / math.sqrt(HD)
    key_slots = key_buffer[:, 0].reshape(window, piece_len, kv_heads, HD)
    value_slots = key_buffer[:, 1].reshape(window, piece_len, kv_heads, HD)
    keys_flat = key_slots.reshape(window * piece_len, kv_heads, HD)
    values_flat = value_slots.reshape(window * piece_len, kv_heads, HD)
    positions = jnp.arange(piece_len, dtype=jnp.int32)
    query_docs = piece_docs(block_doc, piece_index, piece_len)
    query_pos = piece_index * piece_len + positions
    visible_rows = []
    for slot_index in range(window):
        key_index = piece_index - (window - 1) + slot_index
        key_docs = piece_docs(block_doc, key_index, piece_len)
        key_pos = key_index * piece_len + positions
        visible_rows.append(
            (key_docs[None, :] == query_docs[:, None]) & (key_pos[None, :] <= query_pos[:, None])
        )
    visible = jnp.concatenate(visible_rows, axis=1)

    def key_side(form, left, flat):
        return jnp.einsum(form, left, flat, preferred_element_type=jnp.float32)

    def key_sum(form, weights, flat):
        return jnp.einsum(form, weights, flat, preferred_element_type=jnp.float32)

    def per_key(form, weights, right):
        return jnp.einsum(form, weights, right, preferred_element_type=jnp.float32).reshape(
            window, piece_len, kv_heads, HD
        )

    raw_scores = key_side("qhgd,khd->hgqk", query_piece, keys_flat)
    scores = jnp.where(visible[None, None], raw_scores * scaling, masked_score)
    row_max = jnp.max(scores, axis=-1, keepdims=True)
    log_total = row_max + jnp.log(jnp.sum(jnp.exp(scores - row_max), axis=-1, keepdims=True))
    probs = jnp.exp(scores - log_total)
    probs_low = probs.astype(jnp.bfloat16)
    attended = key_sum("hgqk,khd->qhgd", probs_low, values_flat)
    out_low = attended.astype(jnp.bfloat16)
    out_back = lax.optimization_barrier(out_low).astype(jnp.float32)
    delta = jnp.einsum("qhgd,qhgd->hgq", grad_piece.astype(jnp.float32), out_back)
    dprobs = key_side("qhgd,khd->hgqk", grad_piece, values_flat)
    dscores = (probs * (dprobs - delta[..., None])).astype(jnp.bfloat16)
    query_part = (key_sum("hgqk,khd->qhgd", dscores, keys_flat) * scaling).astype(jnp.bfloat16)
    key_part = per_key("hgqk,qhgd->khd", dscores, query_piece) * scaling
    value_part = per_key("hgqk,qhgd->khd", probs_low, grad_piece)
    grads = jnp.stack(
        [
            key_part.reshape(window, piece_len, features),
            value_part.reshape(window, piece_len, features),
        ],
        axis=1,
    )
    return (out_low.reshape(piece_len, -1), query_part.reshape(piece_len, -1), grads)


def local_wide(queries, keys, values, out_grad, block_doc):
    ctx_size = lax.axis_size("ctx")
    my_index = lax.axis_index("ctx")
    reach_back = min(7, ctx_size // 4 - 1)
    window = reach_back + 1
    levels = window.bit_length() - 1
    piece_len = queries.shape[2]
    kv_heads = keys.shape[3] // HD
    group = HQ // HK
    query_all = queries[:, 0].reshape(2, piece_len, kv_heads, group, HD)
    grad_all = out_grad[:, 0].reshape(2, piece_len, kv_heads, group, HD)
    paired = jnp.stack([keys[:, 0], values[:, 0]], axis=1)
    low_buffer = paired[0][None]
    high_buffer = paired[1][None]
    for level_bit in range(levels):
        distance = 1 << level_bit
        low_buffer = jnp.concatenate([move_keys(low_buffer, distance), low_buffer], axis=0)
        high_buffer = jnp.concatenate([move_keys(high_buffer, -distance), high_buffer], axis=0)
    high_index = 2 * ctx_size - 1 - my_index
    low_out, low_qgrad, low_grads = attend(
        query_all[0], grad_all[0], low_buffer, my_index, block_doc
    )
    high_out, high_qgrad, high_grads = attend(
        query_all[1], grad_all[1], high_buffer, high_index, block_doc
    )
    low_back = low_grads
    high_back = high_grads
    for level_bit in reversed(range(levels)):
        distance = 1 << level_bit
        low_back = low_back[distance:] + move_grads(low_back[:distance], -distance)
        high_back = high_back[distance:] + move_grads(high_back[:distance], distance)
    low_total = low_back[0]
    high_total = high_back[0]
    attn_pair = jnp.stack([low_out, high_out])[:, None]
    qgrad_pair = jnp.stack([low_qgrad, high_qgrad])[:, None]
    key_pair = jnp.stack([low_total[0], high_total[0]]).astype(jnp.bfloat16)[:, None]
    value_pair = jnp.stack([low_total[1], high_total[1]]).astype(jnp.bfloat16)[:, None]
    return (attn_pair, qgrad_pair, key_pair, value_pair)


GROUP = HQ // HK
CHUNK = 2 * HD
LOG2_SCALE = math.log2(math.e) / math.sqrt(HD)
SCALE = 1.0 / math.sqrt(HD)
VMEM_LIMIT = 24 * 1024 * 1024

F32 = jnp.float32
BF16 = jnp.bfloat16

in_vmem = pl.BlockSpec(memory_space=pltpu.VMEM)
in_hbm = pl.BlockSpec(memory_space=pltpu.HBM)
in_smem = pl.BlockSpec(memory_space=pltpu.SMEM)


def dot(left, right):
    return jnp.dot(left, right, preferred_element_type=F32)


def dot_t(left, right):
    return lax.dot_general(left, right, (((1,), (1,)), ((), ())), preferred_element_type=F32)


def near_slot():
    return lax.rem(lax.axis_index("ctx"), 2)


def far_slot():
    return 1 - near_slot()


def linked(doc_ref, slot):
    pairs = lax.axis_size("ctx")
    me = lax.axis_index("ctx")
    piece = jnp.where(slot == 0, me, 2 * pairs - 1 - me)
    same = doc_ref[piece] == doc_ref[jnp.maximum(piece - 1, 0)]
    return jnp.where(jnp.logical_and(piece > 0, same), 0.0, masked_score).astype(F32)


def lanes(ref, first, count):
    parts = [ref[:, pl.ds(first + i * HD, HD)] for i in range(count)]
    return jnp.concatenate(parts, axis=0)


def causal(rows, columns):
    key = lax.broadcasted_iota(jnp.int32, (rows, columns), 0)
    query = lax.broadcasted_iota(jnp.int32, (rows, columns), 1)
    return key <= lax.rem(query, rows)


def fetch_pairs(pairs_of_refs, sems):
    copies = [pltpu.make_async_copy(a, b, sems.at[i]) for i, (a, b) in enumerate(pairs_of_refs)]
    for copy in copies:
        copy.start()
    return copies


def pick_kernel(keys, values, far_kv, near_kv, sems):
    far, near = far_slot(), near_slot()
    copies = fetch_pairs(
        [
            (keys.at[far, 0], far_kv.at[0]),
            (values.at[far, 0], far_kv.at[1]),
            (keys.at[near, 0], near_kv.at[0]),
            (values.at[near, 0], near_kv.at[1]),
        ],
        sems,
    )
    for copy in copies:
        copy.wait()


def pick(keys, values):
    _, _, piece_len, features = keys.shape
    shape = pltpu.VMEM((2, piece_len, features), BF16)
    return pl.pallas_call(
        pick_kernel,
        out_shape=(shape, shape),
        in_specs=[in_hbm, in_hbm],
        out_specs=(in_vmem, in_vmem),
        scratch_shapes=[pltpu.SemaphoreType.DMA((4,))],
        name="pick",
    )(keys, values)


def keep_kernel(*refs):
    pass


def keep(far_kv, near_kv):
    shape = pltpu.VMEM(far_kv.shape, BF16)
    return pl.pallas_call(
        keep_kernel,
        out_shape=(shape, shape),
        in_specs=[in_vmem, in_vmem],
        out_specs=(in_vmem, in_vmem),
        input_output_aliases={0: 0, 1: 1},
        cost_estimate=pl.CostEstimate(flops=10**10, bytes_accessed=10**6, transcendentals=0),
        compiler_params=pltpu.CompilerParams(vmem_limit_bytes=VMEM_LIMIT),
        name="keep",
    )(far_kv, near_kv)


def diagonal_kernel(doc, kv, queries, out_grad, weights, dprobs, stats):
    near = near_slot()
    q, do = queries.at[near, 0], out_grad.at[near, 0]
    kv_heads = kv.shape[2] // HD
    bias = linked(doc, near)
    bias_far = linked(doc, 1 - near)
    mask = causal(kv.shape[1], CHUNK)
    for j in range(kv_heads):
        k = kv[0, :, pl.ds(j * HD, HD)]
        v = kv[1, :, pl.ds(j * HD, HD)]
        for h in range(0, GROUP, 2):
            first = (j * GROUP + h) * HD
            at = pl.ds(first, CHUNK)
            logits = jnp.where(mask, dot_t(k, lanes(q, first, 2)) * LOG2_SCALE, masked_score)
            top = jnp.max(logits, axis=0, keepdims=True)
            e = jnp.exp2(logits - top)
            dp = dot_t(v, lanes(do, first, 2))
            weights[:, at] = e
            dprobs[:, at] = dp
            stats[0:1, at] = top
            stats[1:2, at] = jnp.sum(e, axis=0, keepdims=True)
            stats[2:3, at] = jnp.sum(e * dp, axis=0, keepdims=True)
            stats[3:4, at] = jnp.full((1, CHUNK), bias, F32)
            stats[4:5, at] = jnp.full((1, CHUNK), bias_far, F32)


def diagonal(block_doc, kv, queries, out_grad):
    _, _, piece_len, width = queries.shape
    return pl.pallas_call(
        diagonal_kernel,
        out_shape=(
            pltpu.VMEM((piece_len, width), F32),
            pltpu.VMEM((piece_len, width), F32),
            pltpu.VMEM((8, width), F32),
        ),
        in_specs=[in_smem, in_vmem, in_vmem, in_vmem],
        out_specs=(in_vmem,) * 3,
        compiler_params=pltpu.CompilerParams(vmem_limit_bytes=VMEM_LIMIT),
        name="diagonal",
    )(block_doc, kv, queries, out_grad)


def whole_kernel(stats, kv, kv_before, queries, out_grad, before, own, p, ds):
    far = far_slot()
    q, do = queries.at[far, 0], out_grad.at[far, 0]
    kv_heads = kv.shape[2] // HD
    piece_len = kv.shape[1]
    bias = stats[4:5, :CHUNK]
    mask = causal(piece_len, CHUNK)
    for j in range(kv_heads):
        head = pl.ds(j * HD, HD)
        k = jnp.concatenate([kv_before[0, :, head], kv[0, :, head]], axis=0)
        v = jnp.concatenate([kv_before[1, :, head], kv[1, :, head]], axis=0)
        for h in range(0, GROUP, 2):
            first = (j * GROUP + h) * HD
            at = pl.ds(first, CHUNK)
            logits = dot_t(k, lanes(q, first, 2)) * LOG2_SCALE
            cross = logits[:piece_len]
            here = jnp.where(mask, logits[piece_len:], masked_score)
            top = jnp.maximum(
                jnp.max(cross, axis=0, keepdims=True) + bias, jnp.max(here, axis=0, keepdims=True)
            )
            e = jnp.concatenate([jnp.exp2(cross - (top - bias)), jnp.exp2(here - top)], axis=0)
            dp = dot_t(v, lanes(do, first, 2))
            ratio = 1.0 / jnp.sum(e, axis=0, keepdims=True)
            delta = jnp.sum(e * dp, axis=0, keepdims=True) * ratio
            prob = e * ratio
            p[:, at] = prob.astype(BF16)
            ds[:, at] = (prob * (dp - delta)).astype(BF16)
        cols = pl.ds(j * GROUP * HD, GROUP * HD)
        dk = dot(ds[:, cols], lanes(q, j * GROUP * HD, GROUP)) * SCALE
        dv = dot(p[:, cols], lanes(do, j * GROUP * HD, GROUP))
        before[0, :, head] = dk[:piece_len].astype(BF16)
        before[1, :, head] = dv[:piece_len].astype(BF16)
        own[0, :, head] = dk[piece_len:]
        own[1, :, head] = dv[piece_len:]


def whole(stats, kv, kv_before, queries, out_grad):
    _, piece_len, features = kv.shape
    width = queries.shape[3]
    return pl.pallas_call(
        whole_kernel,
        out_shape=(
            pltpu.VMEM((2, piece_len, features), BF16),
            pltpu.VMEM((2, piece_len, features), F32),
            pltpu.VMEM((2 * piece_len, width), BF16),
            pltpu.VMEM((2 * piece_len, width), BF16),
        ),
        in_specs=[in_vmem] * 5,
        out_specs=(in_vmem,) * 4,
        compiler_params=pltpu.CompilerParams(vmem_limit_bytes=VMEM_LIMIT),
        name="whole",
    )(stats, kv, kv_before, queries, out_grad)


def cross_kernel(kv_before, queries, out_grad, stats, before, p, ds, after):
    near = near_slot()
    q, do = queries.at[near, 0], out_grad.at[near, 0]
    piece_len, features = kv_before.shape[1:]
    for j in range(features // HD):
        head = pl.ds(j * HD, HD)
        k = kv_before[0, :, head]
        v = kv_before[1, :, head]
        for h in range(0, GROUP, 2):
            first = (j * GROUP + h) * HD
            at = pl.ds(first, CHUNK)
            top_here, total_here, dot_here, bias = (stats[i : i + 1, at] for i in range(4))
            logits = dot_t(k, lanes(q, first, 2)) * LOG2_SCALE
            top = jnp.maximum(jnp.max(logits, axis=0, keepdims=True) + bias, top_here)
            e = jnp.exp2(logits - (top - bias))
            dp = dot_t(v, lanes(do, first, 2))
            shrink = jnp.exp2(top_here - top)
            ratio = 1.0 / (total_here * shrink + jnp.sum(e, axis=0, keepdims=True))
            delta = (dot_here * shrink + jnp.sum(e * dp, axis=0, keepdims=True)) * ratio
            prob = e * ratio
            p[:, at] = prob.astype(BF16)
            ds[:, at] = (prob * (dp - delta)).astype(BF16)
            after[0:1, at] = shrink * ratio
            after[1:2, at] = delta
        cols = pl.ds(j * GROUP * HD, GROUP * HD)
        dk = dot(ds[:, cols], lanes(q, j * GROUP * HD, GROUP)) * SCALE
        dv = dot(p[:, cols], lanes(do, j * GROUP * HD, GROUP))
        before[0, :, head] = dk.astype(BF16)
        before[1, :, head] = dv.astype(BF16)


def cross(kv_before, queries, out_grad, stats):
    _, piece_len, features = kv_before.shape
    width = queries.shape[3]
    return pl.pallas_call(
        cross_kernel,
        out_shape=(
            pltpu.VMEM((2, piece_len, features), BF16),
            pltpu.VMEM((piece_len, width), BF16),
            pltpu.VMEM((piece_len, width), BF16),
            pltpu.VMEM((8, width), F32),
        ),
        in_specs=[in_vmem] * 4,
        out_specs=(in_vmem,) * 4,
        compiler_params=pltpu.CompilerParams(vmem_limit_bytes=VMEM_LIMIT),
        name="cross",
    )(kv_before, queries, out_grad, stats)


def turn(wide, ref, first):
    for i in range(wide.shape[1] // HD):
        ref[:, pl.ds(first + i * HD, HD)] = wide[:, i * HD : (i + 1) * HD].T


def rest_kernel(
    near_kv, next_kv, queries, out_grad, weights, dprobs, p_next, ds_next, after, passed, far_kv, mate_kv,
    p_far, ds_far, out, q_grad, k_grad, v_grad, o, dq, p, ds, dk_low, dv_low, sems,
):
    near, far = near_slot(), far_slot()
    q, do = queries.at[near, 0], out_grad.at[near, 0]
    kv_heads = near_kv.shape[2] // HD
    span = GROUP * HD
    backs = []

    def give_back(side, slot, j):
        cols = pl.ds(j * span, span)
        for n, (a, b) in enumerate(((o, out), (dq, q_grad))):
            sem = sems.at[2 + (side * kv_heads + j) * 2 + n]
            back = pltpu.make_async_copy(a.at[side, :, cols], b.at[slot, 0, :, cols], sem)
            back.start()
            backs.append(back)

    for j in range(kv_heads):
        head = pl.ds(j * HD, HD)
        k_t = jnp.concatenate([mate_kv[0, :, head], far_kv[0, :, head]], axis=0).T
        v_t = jnp.concatenate([mate_kv[1, :, head], far_kv[1, :, head]], axis=0).T
        for h in range(0, GROUP, 2):
            first = (j * GROUP + h) * HD
            at = pl.ds(first, CHUNK)
            turn(dot(v_t, p_far[:, at]).astype(BF16), o.at[1], first)
            turn((dot(k_t, ds_far[:, at]) * SCALE).astype(BF16), dq.at[1], first)
        give_back(1, far, j)
    for j in range(kv_heads):
        head = pl.ds(j * HD, HD)
        k_t = jnp.concatenate([next_kv[0, :, head], near_kv[0, :, head]], axis=0).T
        v_t = jnp.concatenate([next_kv[1, :, head], near_kv[1, :, head]], axis=0).T
        for h in range(0, GROUP, 2):
            first = (j * GROUP + h) * HD
            at = pl.ds(first, CHUNK)
            prob = weights[:, at] * after[0:1, at]
            prob_low = prob.astype(BF16)
            ds_low = (prob * (dprobs[:, at] - after[1:2, at])).astype(BF16)
            p[:, pl.ds(h * HD, CHUNK)] = prob_low
            ds[:, pl.ds(h * HD, CHUNK)] = ds_low
            turn(dot(v_t, jnp.concatenate([p_next[:, at], prob_low], axis=0)).astype(BF16), o.at[0], first)
            dq_t = dot(k_t, jnp.concatenate([ds_next[:, at], ds_low], axis=0)) * SCALE
            turn(dq_t.astype(BF16), dq.at[0], first)
        give_back(0, near, j)
        dk = dot(ds[...], lanes(q, j * span, GROUP)) * SCALE
        dv = dot(p[...], lanes(do, j * span, GROUP))
        dk_low[:, head] = (dk + passed[0, :, head].astype(F32)).astype(BF16)
        dv_low[:, head] = (dv + passed[1, :, head].astype(F32)).astype(BF16)
    backs += fetch_pairs([(dk_low, k_grad.at[near, 0]), (dv_low, v_grad.at[near, 0])], sems)
    for back in backs:
        back.wait()


def rest(*operands, shape):
    _, piece_len, features = operands[0].shape
    width = shape[3]
    kv_heads = features // HD
    wide = jax.ShapeDtypeStruct(shape, BF16)
    small = jax.ShapeDtypeStruct(shape[:3] + (features,), BF16)
    return pl.pallas_call(
        rest_kernel,
        out_shape=(wide, wide, small, small),
        in_specs=[in_vmem] * len(operands),
        out_specs=(in_hbm,) * 4,
        scratch_shapes=[pltpu.VMEM((2, piece_len, width), BF16)] * 2
        + [pltpu.VMEM((piece_len, GROUP * HD), BF16)] * 2
        + [pltpu.VMEM((piece_len, features), BF16)] * 2
        + [pltpu.SemaphoreType.DMA((2 + 4 * kv_heads,))],
        compiler_params=pltpu.CompilerParams(vmem_limit_bytes=VMEM_LIMIT),
        name="rest",
    )(*operands)


def total_kernel(own, passed, k_grad_in, v_grad_in, k_grad, v_grad, low, sems):
    far = far_slot()
    low[...] = (own[...] + passed[...].astype(F32)).astype(BF16)
    copies = fetch_pairs([(low.at[0], k_grad.at[far, 0]), (low.at[1], v_grad.at[far, 0])], sems)
    for copy in copies:
        copy.wait()


def total(own, passed, k_grad, v_grad):
    return pl.pallas_call(
        total_kernel,
        out_shape=(jax.ShapeDtypeStruct(k_grad.shape, BF16),) * 2,
        in_specs=[in_vmem] * 2 + [in_hbm] * 2,
        out_specs=(in_hbm,) * 2,
        input_output_aliases={2: 0, 3: 1},
        scratch_shapes=[pltpu.VMEM(own.shape, BF16), pltpu.SemaphoreType.DMA((2,))],
        compiler_params=pltpu.CompilerParams(vmem_limit_bytes=VMEM_LIMIT),
        name="total",
    )(own, passed, k_grad, v_grad)


def complete(route, pairs, flip=False):
    sources = [i for i in range(pairs) if i not in {a for a, _ in route}]
    targets = [i for i in range(pairs) if i not in {b for _, b in route}]
    spare = [(i, i ^ 1) for i in sources if i ^ 1 in targets]
    sources = [i for i in sources if i not in {a for a, _ in spare}]
    targets = [i for i in targets if i not in {b for _, b in spare}]
    if flip:
        targets = targets[::-1]
    for turn_by in range(max(1, len(targets))):
        turned = targets[turn_by:] + targets[:turn_by]
        if all(a != b for a, b in zip(sources, turned)):
            return route + spare + list(zip(sources, turned))
    return route


def local_pairs(queries, keys, values, out_grad, block_doc):
    pairs = lax.axis_size("ctx")
    mates = [(i, i ^ 1) for i in range(pairs) if i ^ 1 < pairs]
    low_route = [(i, i + 1) for i in range(3, pairs - 1, 2)]
    high_route = [(i + 1, i) for i in range(1, pairs - 3, 2)]
    links = low_route + high_route
    route = complete(links, pairs)
    route_back = complete([(b, a) for a, b in links], pairs, flip=True)
    far_kv, near_kv = keep(*pick(keys, values))
    mate_kv = lax.ppermute(near_kv, "ctx", mates)
    next_kv = lax.ppermute(far_kv, "ctx", route)
    weights, dprobs, stats = diagonal(block_doc, near_kv, queries, out_grad)
    mate_grads, own_grads, p_far, ds_far = whole(stats, far_kv, mate_kv, queries, out_grad)
    mate_back = lax.ppermute(mate_grads, "ctx", mates)
    next_grads, p_next, ds_next, after = cross(next_kv, queries, out_grad, stats)
    next_back = lax.ppermute(next_grads, "ctx", route_back)
    out, q_grad, k_grad, v_grad = rest(
        near_kv, next_kv, queries, out_grad, weights, dprobs, p_next, ds_next, after, mate_back,
        far_kv, mate_kv, p_far, ds_far, shape=queries.shape,
    )
    k_grad, v_grad = total(own_grads, next_back, k_grad, v_grad)
    return (out, q_grad, k_grad, v_grad)


def local(queries, keys, values, out_grad, block_doc):
    window = min(7, lax.axis_size("ctx") // 4 - 1) + 1
    piece_len = queries.shape[2]
    if window == 2 and piece_len == BLOCK:
        return local_pairs(queries, keys, values, out_grad, block_doc)
    return local_wide(queries, keys, values, out_grad, block_doc)


def solution(mesh):
    in_specs = (
        P(None, "ctx", None, "tp"),
        P(None, "ctx", None, "tp"),
        P(None, "ctx", None, "tp"),
        P(None, "ctx", None, "tp"),
        P(),
    )
    out_specs = (
        P(None, "ctx", None, "tp"),
        P(None, "ctx", None, "tp"),
        P(None, "ctx", None, "tp"),
        P(None, "ctx", None, "tp"),
    )
    return jax.shard_map(local, mesh=mesh, in_specs=in_specs, out_specs=out_specs, check_vma=False)
```

```python
import functools
import math

import jax
import jax.numpy as jnp
from jax import lax
from jax.experimental import pallas as pl
from jax.experimental.pallas import tpu as pltpu
from jax.sharding import PartitionSpec as P

HQ = 64
HK = 8
HD = 128
BLOCK = 128


masked_score = -1e30


def shifted(block, axis, distance):
    devices = range(lax.axis_size(axis))
    route = [(i - distance, i) for i in devices if i - distance in devices]
    return lax.ppermute(block, axis, route)


def move_keys(payload, distance):
    return shifted(payload, "ctx", distance)


def move_grads(payload, distance):
    return shifted(payload.astype(jnp.bfloat16), "ctx", distance).astype(payload.dtype)


def piece_docs(block_doc, piece_index, piece_len):
    per_piece = piece_len // BLOCK
    start = jnp.maximum(piece_index, 0) * per_piece
    doc_blocks = lax.dynamic_slice_in_dim(block_doc, start, per_piece, 0)
    doc_tokens = jnp.repeat(doc_blocks, BLOCK)
    return jnp.where(piece_index >= 0, doc_tokens, -1)


def attend(query_piece, grad_piece, key_buffer, piece_index, block_doc):
    window, _, piece_len, features = key_buffer.shape
    kv_heads = features // HD
    scaling = 1.0 / math.sqrt(HD)
    key_slots = key_buffer[:, 0].reshape(window, piece_len, kv_heads, HD)
    value_slots = key_buffer[:, 1].reshape(window, piece_len, kv_heads, HD)
    keys_flat = key_slots.reshape(window * piece_len, kv_heads, HD)
    values_flat = value_slots.reshape(window * piece_len, kv_heads, HD)
    positions = jnp.arange(piece_len, dtype=jnp.int32)
    query_docs = piece_docs(block_doc, piece_index, piece_len)
    query_pos = piece_index * piece_len + positions
    visible_rows = []
    for slot_index in range(window):
        key_index = piece_index - (window - 1) + slot_index
        key_docs = piece_docs(block_doc, key_index, piece_len)
        key_pos = key_index * piece_len + positions
        visible_rows.append(
            (key_docs[None, :] == query_docs[:, None]) & (key_pos[None, :] <= query_pos[:, None])
        )
    visible = jnp.concatenate(visible_rows, axis=1)

    def key_side(form, left, flat):
        return jnp.einsum(form, left, flat, preferred_element_type=jnp.float32)

    def key_sum(form, weights, flat):
        return jnp.einsum(form, weights, flat, preferred_element_type=jnp.float32)

    def per_key(form, weights, right):
        return jnp.einsum(form, weights, right, preferred_element_type=jnp.float32).reshape(
            window, piece_len, kv_heads, HD
        )

    raw_scores = key_side("qhgd,khd->hgqk", query_piece, keys_flat)
    scores = jnp.where(visible[None, None], raw_scores * scaling, masked_score)
    row_max = jnp.max(scores, axis=-1, keepdims=True)
    log_total = row_max + jnp.log(jnp.sum(jnp.exp(scores - row_max), axis=-1, keepdims=True))
    probs = jnp.exp(scores - log_total)
    probs_low = probs.astype(jnp.bfloat16)
    attended = key_sum("hgqk,khd->qhgd", probs_low, values_flat)
    out_low = attended.astype(jnp.bfloat16)
    out_back = lax.optimization_barrier(out_low).astype(jnp.float32)
    delta = jnp.einsum("qhgd,qhgd->hgq", grad_piece.astype(jnp.float32), out_back)
    dprobs = key_side("qhgd,khd->hgqk", grad_piece, values_flat)
    dscores = (probs * (dprobs - delta[..., None])).astype(jnp.bfloat16)
    query_part = (key_sum("hgqk,khd->qhgd", dscores, keys_flat) * scaling).astype(jnp.bfloat16)
    key_part = per_key("hgqk,qhgd->khd", dscores, query_piece) * scaling
    value_part = per_key("hgqk,qhgd->khd", probs_low, grad_piece)
    grads = jnp.stack(
        [
            key_part.reshape(window, piece_len, features),
            value_part.reshape(window, piece_len, features),
        ],
        axis=1,
    )
    return (out_low.reshape(piece_len, -1), query_part.reshape(piece_len, -1), grads)


def local_wide(queries, keys, values, out_grad, block_doc):
    ctx_size = lax.axis_size("ctx")
    my_index = lax.axis_index("ctx")
    reach_back = min(7, ctx_size // 4 - 1)
    window = reach_back + 1
    levels = window.bit_length() - 1
    piece_len = queries.shape[2]
    kv_heads = keys.shape[3] // HD
    group = HQ // HK
    query_all = queries[:, 0].reshape(2, piece_len, kv_heads, group, HD)
    grad_all = out_grad[:, 0].reshape(2, piece_len, kv_heads, group, HD)
    paired = jnp.stack([keys[:, 0], values[:, 0]], axis=1)
    low_buffer = paired[0][None]
    high_buffer = paired[1][None]
    for level_bit in range(levels):
        distance = 1 << level_bit
        low_buffer = jnp.concatenate([move_keys(low_buffer, distance), low_buffer], axis=0)
        high_buffer = jnp.concatenate([move_keys(high_buffer, -distance), high_buffer], axis=0)
    high_index = 2 * ctx_size - 1 - my_index
    low_out, low_qgrad, low_grads = attend(
        query_all[0], grad_all[0], low_buffer, my_index, block_doc
    )
    high_out, high_qgrad, high_grads = attend(
        query_all[1], grad_all[1], high_buffer, high_index, block_doc
    )
    low_back = low_grads
    high_back = high_grads
    for level_bit in reversed(range(levels)):
        distance = 1 << level_bit
        low_back = low_back[distance:] + move_grads(low_back[:distance], -distance)
        high_back = high_back[distance:] + move_grads(high_back[:distance], distance)
    low_total = low_back[0]
    high_total = high_back[0]
    attn_pair = jnp.stack([low_out, high_out])[:, None]
    qgrad_pair = jnp.stack([low_qgrad, high_qgrad])[:, None]
    key_pair = jnp.stack([low_total[0], high_total[0]]).astype(jnp.bfloat16)[:, None]
    value_pair = jnp.stack([low_total[1], high_total[1]]).astype(jnp.bfloat16)[:, None]
    return (attn_pair, qgrad_pair, key_pair, value_pair)


GROUP = HQ // HK
CHUNK = 2 * HD
LOG2_SCALE = math.log2(math.e) / math.sqrt(HD)
SCALE = 1.0 / math.sqrt(HD)
VMEM_LIMIT = 24 * 1024 * 1024

F32 = jnp.float32
BF16 = jnp.bfloat16

in_vmem = pl.BlockSpec(memory_space=pltpu.VMEM)
in_hbm = pl.BlockSpec(memory_space=pltpu.HBM)
in_smem = pl.BlockSpec(memory_space=pltpu.SMEM)


def dot(left, right):
    return jnp.dot(left, right, preferred_element_type=F32)


def dot_t(left, right):
    return lax.dot_general(left, right, (((1,), (1,)), ((), ())), preferred_element_type=F32)


def near_slot():
    return lax.rem(lax.axis_index("ctx"), 2)


def far_slot():
    return 1 - near_slot()


def linked(doc_ref, slot):
    pairs = lax.axis_size("ctx")
    me = lax.axis_index("ctx")
    piece = jnp.where(slot == 0, me, 2 * pairs - 1 - me)
    same = doc_ref[piece] == doc_ref[jnp.maximum(piece - 1, 0)]
    return jnp.where(jnp.logical_and(piece > 0, same), 0.0, masked_score).astype(F32)


def lanes(ref, first, count):
    parts = [ref[:, pl.ds(first + i * HD, HD)] for i in range(count)]
    return jnp.concatenate(parts, axis=0)


def causal(rows, columns):
    key = lax.broadcasted_iota(jnp.int32, (rows, columns), 0)
    query = lax.broadcasted_iota(jnp.int32, (rows, columns), 1)
    return key <= lax.rem(query, rows)


def fetch_pairs(pairs_of_refs, sems):
    copies = [pltpu.make_async_copy(a, b, sems.at[i]) for i, (a, b) in enumerate(pairs_of_refs)]
    for copy in copies:
        copy.start()
    return copies


def pick_kernel(needed, keys, values, block_doc, far_kv, near_kv, case, doc, sems):
    far, near = far_slot(), near_slot()
    copies = fetch_pairs(
        [
            (block_doc, doc),
            (keys.at[far, 0], far_kv.at[0]),
            (values.at[far, 0], far_kv.at[1]),
            (keys.at[near, 0], near_kv.at[0]),
            (values.at[near, 0], near_kv.at[1]),
        ],
        sems,
    )
    copies[0].wait()
    case[0] = needed(doc)
    for copy in copies[1:]:
        copy.wait()


def pick(keys, values, block_doc, needed):
    _, _, piece_len, features = keys.shape
    shape = pltpu.VMEM((2, piece_len, features), BF16)
    return pl.pallas_call(
        functools.partial(pick_kernel, needed),
        out_shape=(
            shape,
            shape,
            pltpu.SMEM((1,), jnp.int32),
            pltpu.SMEM(block_doc.shape, jnp.int32),
        ),
        in_specs=[in_hbm, in_hbm, in_hbm],
        out_specs=(in_vmem, in_vmem, in_smem, in_smem),
        scratch_shapes=[pltpu.SemaphoreType.DMA((5,))],
        name="pick",
    )(keys, values, block_doc)


def keep_kernel(*refs):
    pass


def keep(far_kv, near_kv):
    shape = pltpu.VMEM(far_kv.shape, BF16)
    return pl.pallas_call(
        keep_kernel,
        out_shape=(shape, shape),
        in_specs=[in_vmem, in_vmem],
        out_specs=(in_vmem, in_vmem),
        input_output_aliases={0: 0, 1: 1},
        cost_estimate=pl.CostEstimate(flops=10**10, bytes_accessed=10**6, transcendentals=0),
        compiler_params=pltpu.CompilerParams(vmem_limit_bytes=VMEM_LIMIT),
        name="keep",
    )(far_kv, near_kv)


def diagonal_kernel(doc, kv, queries, out_grad, weights, dprobs, stats):
    near = near_slot()
    q, do = queries.at[near, 0], out_grad.at[near, 0]
    kv_heads = kv.shape[2] // HD
    bias = linked(doc, near)
    bias_far = linked(doc, 1 - near)
    mask = causal(kv.shape[1], CHUNK)
    for j in range(kv_heads):
        k = kv[0, :, pl.ds(j * HD, HD)]
        v = kv[1, :, pl.ds(j * HD, HD)]
        for h in range(0, GROUP, 2):
            first = (j * GROUP + h) * HD
            at = pl.ds(first, CHUNK)
            logits = jnp.where(mask, dot_t(k, lanes(q, first, 2)) * LOG2_SCALE, masked_score)
            top = jnp.max(logits, axis=0, keepdims=True)
            e = jnp.exp2(logits - top)
            dp = dot_t(v, lanes(do, first, 2))
            weights[:, at] = e
            dprobs[:, at] = dp
            stats[0:1, at] = top
            stats[1:2, at] = jnp.sum(e, axis=0, keepdims=True)
            stats[2:3, at] = jnp.sum(e * dp, axis=0, keepdims=True)
            stats[3:4, at] = jnp.full((1, CHUNK), bias, F32)
            stats[4:5, at] = jnp.full((1, CHUNK), bias_far, F32)


def diagonal(block_doc, kv, queries, out_grad):
    _, _, piece_len, width = queries.shape
    return pl.pallas_call(
        diagonal_kernel,
        out_shape=(
            pltpu.VMEM((piece_len, width), F32),
            pltpu.VMEM((piece_len, width), F32),
            pltpu.VMEM((8, width), F32),
        ),
        in_specs=[in_smem, in_vmem, in_vmem, in_vmem],
        out_specs=(in_vmem,) * 3,
        compiler_params=pltpu.CompilerParams(vmem_limit_bytes=VMEM_LIMIT),
        name="diagonal",
    )(block_doc, kv, queries, out_grad)


def whole_kernel(stats, kv, kv_before, queries, out_grad, before, own, p, ds):
    far = far_slot()
    q, do = queries.at[far, 0], out_grad.at[far, 0]
    kv_heads = kv.shape[2] // HD
    piece_len = kv.shape[1]
    bias = stats[4:5, :CHUNK]
    mask = causal(piece_len, CHUNK)
    for j in range(kv_heads):
        head = pl.ds(j * HD, HD)
        k = jnp.concatenate([kv_before[0, :, head], kv[0, :, head]], axis=0)
        v = jnp.concatenate([kv_before[1, :, head], kv[1, :, head]], axis=0)
        for h in range(0, GROUP, 2):
            first = (j * GROUP + h) * HD
            at = pl.ds(first, CHUNK)
            logits = dot_t(k, lanes(q, first, 2)) * LOG2_SCALE
            cross = logits[:piece_len]
            here = jnp.where(mask, logits[piece_len:], masked_score)
            top = jnp.maximum(
                jnp.max(cross, axis=0, keepdims=True) + bias, jnp.max(here, axis=0, keepdims=True)
            )
            e = jnp.concatenate([jnp.exp2(cross - (top - bias)), jnp.exp2(here - top)], axis=0)
            dp = dot_t(v, lanes(do, first, 2))
            ratio = 1.0 / jnp.sum(e, axis=0, keepdims=True)
            delta = jnp.sum(e * dp, axis=0, keepdims=True) * ratio
            prob = e * ratio
            p[:, at] = prob.astype(BF16)
            ds[:, at] = (prob * (dp - delta)).astype(BF16)
        cols = pl.ds(j * GROUP * HD, GROUP * HD)
        dk = dot(ds[:, cols], lanes(q, j * GROUP * HD, GROUP)) * SCALE
        dv = dot(p[:, cols], lanes(do, j * GROUP * HD, GROUP))
        before[0, :, head] = dk[:piece_len].astype(BF16)
        before[1, :, head] = dv[:piece_len].astype(BF16)
        own[0, :, head] = dk[piece_len:]
        own[1, :, head] = dv[piece_len:]


def whole(stats, kv, kv_before, queries, out_grad):
    _, piece_len, features = kv.shape
    width = queries.shape[3]
    return pl.pallas_call(
        whole_kernel,
        out_shape=(
            pltpu.VMEM((2, piece_len, features), BF16),
            pltpu.VMEM((2, piece_len, features), F32),
            pltpu.VMEM((2 * piece_len, width), BF16),
            pltpu.VMEM((2 * piece_len, width), BF16),
        ),
        in_specs=[in_vmem] * 5,
        out_specs=(in_vmem,) * 4,
        compiler_params=pltpu.CompilerParams(vmem_limit_bytes=VMEM_LIMIT),
        name="whole",
    )(stats, kv, kv_before, queries, out_grad)


def cross_kernel(kv_before, queries, out_grad, stats, behind, before, p, ds, after):
    near = near_slot()
    q, do = queries.at[near, 0], out_grad.at[near, 0]
    piece_len, features = kv_before.shape[1:]
    seen = jnp.max(stats[3:4, :HD]) == 0.0

    @pl.when(seen)
    def _():
        for j in range(features // HD):
            head = pl.ds(j * HD, HD)
            k = kv_before[0, :, head]
            v = kv_before[1, :, head]
            for h in range(0, GROUP, 2):
                first = (j * GROUP + h) * HD
                at = pl.ds(first, CHUNK)
                top_here, total_here, dot_here = (stats[i : i + 1, at] for i in range(3))
                logits = dot_t(k, lanes(q, first, 2)) * LOG2_SCALE
                top = jnp.maximum(jnp.max(logits, axis=0, keepdims=True), top_here)
                e = jnp.exp2(logits - top)
                dp = dot_t(v, lanes(do, first, 2))
                shrink = jnp.exp2(top_here - top)
                ratio = 1.0 / (total_here * shrink + jnp.sum(e, axis=0, keepdims=True))
                delta = (dot_here * shrink + jnp.sum(e * dp, axis=0, keepdims=True)) * ratio
                prob = e * ratio
                p[:, at] = prob.astype(BF16)
                ds[:, at] = (prob * (dp - delta)).astype(BF16)
                after[0:1, at] = shrink * ratio
                after[1:2, at] = delta
            cols = pl.ds(j * GROUP * HD, GROUP * HD)
            dk = dot(ds[:, cols], lanes(q, j * GROUP * HD, GROUP)) * SCALE
            dv = dot(p[:, cols], lanes(do, j * GROUP * HD, GROUP))
            before[0, :, head] = dk.astype(BF16)
            before[1, :, head] = dv.astype(BF16)

    @pl.when(jnp.logical_not(seen))
    def _():
        before[...] = jnp.zeros_like(before)
        p[...] = jnp.zeros_like(p)
        ds[...] = jnp.zeros_like(ds)
        ratio = 1.0 / stats[1:2, :]
        after[0:1, :] = ratio
        after[1:2, :] = stats[2:3, :] * ratio


def cross(kv_before, queries, out_grad, stats, behind):
    _, piece_len, features = kv_before.shape
    width = queries.shape[3]
    return pl.pallas_call(
        cross_kernel,
        out_shape=(
            pltpu.VMEM((2, piece_len, features), BF16),
            pltpu.VMEM((piece_len, width), BF16),
            pltpu.VMEM((piece_len, width), BF16),
            pltpu.VMEM((8, width), F32),
        ),
        in_specs=[in_vmem] * 5,
        out_specs=(in_vmem,) * 4,
        compiler_params=pltpu.CompilerParams(vmem_limit_bytes=VMEM_LIMIT),
        name="cross",
    )(kv_before, queries, out_grad, stats, behind)


def turn(wide, ref, first):
    for i in range(wide.shape[1] // HD):
        ref[:, pl.ds(first + i * HD, HD)] = wide[:, i * HD : (i + 1) * HD].T


def rest_kernel(alone, *refs):
    near_kv, queries, out_grad, weights, dprobs, after, far_kv, mate_kv, p_far, ds_far = refs[:10]
    if not alone:
        next_kv, p_next, ds_next = refs[10:13]
    out, q_grad, own, o, dq, p, ds, sems = refs[-8:]
    near, far = near_slot(), far_slot()
    q, do = queries.at[near, 0], out_grad.at[near, 0]
    kv_heads = near_kv.shape[2] // HD
    span = GROUP * HD
    backs = []

    def give_back(side, slot, j):
        cols = pl.ds(j * span, span)
        for n, (a, b) in enumerate(((o, out), (dq, q_grad))):
            sem = sems.at[(side * kv_heads + j) * 2 + n]
            back = pltpu.make_async_copy(a.at[side, :, cols], b.at[slot, 0, :, cols], sem)
            back.start()
            backs.append(back)

    for j in range(kv_heads):
        head = pl.ds(j * HD, HD)
        k_t = jnp.concatenate([mate_kv[0, :, head], far_kv[0, :, head]], axis=0).T
        v_t = jnp.concatenate([mate_kv[1, :, head], far_kv[1, :, head]], axis=0).T
        for h in range(0, GROUP, 2):
            first = (j * GROUP + h) * HD
            at = pl.ds(first, CHUNK)
            turn(dot(v_t, p_far[:, at]).astype(BF16), o.at[1], first)
            turn((dot(k_t, ds_far[:, at]) * SCALE).astype(BF16), dq.at[1], first)
        give_back(1, far, j)
    for j in range(kv_heads):
        head = pl.ds(j * HD, HD)
        if alone:
            k_t, v_t = near_kv[0, :, head].T, near_kv[1, :, head].T
        else:
            k_t = jnp.concatenate([next_kv[0, :, head], near_kv[0, :, head]], axis=0).T
            v_t = jnp.concatenate([next_kv[1, :, head], near_kv[1, :, head]], axis=0).T
        for h in range(0, GROUP, 2):
            first = (j * GROUP + h) * HD
            at = pl.ds(first, CHUNK)
            if alone:
                ratio = 1.0 / after[1:2, at]
                delta = after[2:3, at] * ratio
            else:
                ratio, delta = after[0:1, at], after[1:2, at]
            prob = weights[:, at] * ratio
            prob_low = prob.astype(BF16)
            ds_low = (prob * (dprobs[:, at] - delta)).astype(BF16)
            p[:, pl.ds(h * HD, CHUNK)] = prob_low
            ds[:, pl.ds(h * HD, CHUNK)] = ds_low
            if not alone:
                prob_low = jnp.concatenate([p_next[:, at], prob_low], axis=0)
                ds_low = jnp.concatenate([ds_next[:, at], ds_low], axis=0)
            turn(dot(v_t, prob_low).astype(BF16), o.at[0], first)
            turn((dot(k_t, ds_low) * SCALE).astype(BF16), dq.at[0], first)
        give_back(0, near, j)
        own[0, :, head] = dot(ds[...], lanes(q, j * span, GROUP)) * SCALE
        own[1, :, head] = dot(p[...], lanes(do, j * span, GROUP))
    for back in backs:
        back.wait()


def rest(alone, *operands, shape):
    _, piece_len, features = operands[0].shape
    width = shape[3]
    kv_heads = features // HD
    wide = pltpu.HBM(shape, BF16)
    return pl.pallas_call(
        functools.partial(rest_kernel, alone),
        out_shape=(wide, wide, pltpu.VMEM((2, piece_len, features), F32)),
        in_specs=[in_vmem] * len(operands),
        out_specs=(in_hbm, in_hbm, in_vmem),
        scratch_shapes=[pltpu.VMEM((2, piece_len, width), BF16)] * 2
        + [pltpu.VMEM((piece_len, GROUP * HD), BF16)] * 2
        + [pltpu.SemaphoreType.DMA((4 * kv_heads,))],
        compiler_params=pltpu.CompilerParams(vmem_limit_bytes=VMEM_LIMIT),
        name="rest",
    )(*operands)


def total_kernel(near_own, far_own, near_back, *refs):
    k_grad, v_grad, k_low, v_low, sems = refs[-5:]
    near, far = near_slot(), far_slot()
    for n, low in enumerate((k_low, v_low)):
        low[near, 0] = (near_own[n] + near_back[n].astype(F32)).astype(BF16)
        mine = far_own[n]
        if len(refs) > 5:
            mine = mine + refs[0][n].astype(F32)
        low[far, 0] = mine.astype(BF16)
    for copy in fetch_pairs([(k_low, k_grad), (v_low, v_grad)], sems):
        copy.wait()


def total(*operands):
    _, piece_len, features = operands[0].shape
    shape = (2, 1, piece_len, features)
    return pl.pallas_call(
        total_kernel,
        out_shape=(pltpu.HBM(shape, BF16),) * 2,
        in_specs=[in_vmem] * len(operands),
        out_specs=(in_hbm,) * 2,
        scratch_shapes=[pltpu.VMEM(shape, BF16)] * 2 + [pltpu.SemaphoreType.DMA((2,))],
        compiler_params=pltpu.CompilerParams(vmem_limit_bytes=VMEM_LIMIT),
        name="total",
    )(*operands)


def complete(route, pairs, spare):
    def whole_turn(routes):
        ends = [sorted(side) for side in zip(*routes)]
        return ends == [list(range(pairs))] * 2 and all(a != b for a, b in routes)

    if whole_turn(route + spare):
        return route + spare
    sources = [i for i in range(pairs) if i not in {a for a, _ in route}]
    targets = [i for i in range(pairs) if i not in {b for _, b in route}]
    for turn_by in range(len(targets)):
        filled = route + list(zip(sources, targets[turn_by:] + targets[:turn_by]))
        if whole_turn(filled):
            return filled
    return route


def far_links(pairs):
    low = [(i, i + 1, i) for i in range(3, pairs - 1, 2)]
    high = [(i + 1, i, 2 * pairs - 2 - i) for i in range(1, pairs - 3, 2)]
    return low + high


def is_outer(link):
    return min(link[0], link[1]) % 4 == 3


SPARE = {
    "both": [(1, 0), (6, 7), (0, 2), (7, 5)],
    "both back": [(0, 1), (7, 6), (2, 7), (5, 0)],
    "outer": [(2, 6), (6, 7), (7, 5), (5, 1), (1, 0), (0, 2)],
    "outer back": [(2, 6), (6, 7), (7, 5), (5, 1), (1, 0), (0, 2)],
    "inner": [(3, 2), (4, 5), (6, 7), (1, 0), (0, 3), (7, 4)],
    "inner back": [(2, 3), (5, 4), (7, 6), (0, 1), (3, 0), (4, 7)],
}


def attend_pairs(links, name, queries, out_grad, doc, far_kv, near_kv):
    pairs = lax.axis_size("ctx")
    mates = [(i, i ^ 1) for i in range(pairs) if i ^ 1 < pairs]
    flows = [(a, b) for a, b, _ in links]
    far_kv, near_kv = keep(far_kv, near_kv)
    mate_kv = lax.ppermute(near_kv, "ctx", mates)
    if links:
        next_kv = lax.ppermute(far_kv, "ctx", complete(flows, pairs, SPARE[name]))
    weights, dprobs, stats = diagonal(doc, near_kv, queries, out_grad)
    mate_grads, far_own, p_far, ds_far = whole(stats, far_kv, mate_kv, queries, out_grad)
    mate_back = lax.ppermute(mate_grads, "ctx", mates)
    after, more, far_back = stats, (), ()
    if links:
        next_grads, p_next, ds_next, after = cross(
            next_kv, queries, out_grad, stats, mate_grads
        )
        more = (next_kv, p_next, ds_next)
        back = [(b, a) for a, b in flows]
        far_back = (
            lax.ppermute(next_grads, "ctx", complete(back, pairs, SPARE[name + " back"])),
        )
    out, q_grad, near_own = rest(
        not links, near_kv, queries, out_grad, weights, dprobs, after, far_kv, mate_kv, p_far,
        ds_far, *more, shape=queries.shape,
    )
    k_grad, v_grad = total(near_own, far_own, mate_back, *far_back)
    return (out, q_grad, k_grad, v_grad)


def local_pairs(queries, keys, values, out_grad, block_doc):
    links = far_links(lax.axis_size("ctx"))
    outer = [link for link in links if is_outer(link)]
    inner = [link for link in links if not is_outer(link)]

    def needed(doc):
        def any_linked(some):
            same = [doc[first] == doc[first + 1] for _, _, first in some]
            return functools.reduce(jnp.logical_or, same)

        return jnp.where(any_linked(inner), 1, 0) + jnp.where(any_linked(outer), 2, 0)

    far_kv, near_kv, case, doc = pick(keys, values, block_doc, needed)
    cases = (([], "none"), (inner, "inner"), (outer, "outer"), (links, "both"))
    return lax.switch(
        case[0],
        [functools.partial(attend_pairs, some, name) for some, name in cases],
        queries, out_grad, doc, far_kv, near_kv,
    )


def local(queries, keys, values, out_grad, block_doc):
    window = min(7, lax.axis_size("ctx") // 4 - 1) + 1
    piece_len = queries.shape[2]
    even = lax.axis_size("ctx") % 2 == 0
    if window == 2 and piece_len == BLOCK and even:
        return local_pairs(queries, keys, values, out_grad, block_doc)
    return local_wide(queries, keys, values, out_grad, block_doc)


def solution(mesh):
    in_specs = (
        P(None, "ctx", None, "tp"),
        P(None, "ctx", None, "tp"),
        P(None, "ctx", None, "tp"),
        P(None, "ctx", None, "tp"),
        P(),
    )
    out_specs = (
        P(None, "ctx", None, "tp"),
        P(None, "ctx", None, "tp"),
        P(None, "ctx", None, "tp"),
        P(None, "ctx", None, "tp"),
    )
    return jax.shard_map(local, mesh=mesh, in_specs=in_specs, out_specs=out_specs, check_vma=False)
```

```python
import functools
import math

import jax
import jax.numpy as jnp
from jax import lax
from jax.experimental import pallas as pl
from jax.experimental.pallas import tpu as pltpu
from jax.sharding import PartitionSpec as P

HQ = 64
HK = 8
HD = 128
BLOCK = 128


masked_score = -1e30


def shifted(block, axis, distance):
    devices = range(lax.axis_size(axis))
    route = [(i - distance, i) for i in devices if i - distance in devices]
    return lax.ppermute(block, axis, route)


def move_keys(payload, distance):
    return shifted(payload, "ctx", distance)


def move_grads(payload, distance):
    return shifted(payload.astype(jnp.bfloat16), "ctx", distance).astype(payload.dtype)


def piece_docs(block_doc, piece_index, piece_len):
    per_piece = piece_len // BLOCK
    start = jnp.maximum(piece_index, 0) * per_piece
    doc_blocks = lax.dynamic_slice_in_dim(block_doc, start, per_piece, 0)
    doc_tokens = jnp.repeat(doc_blocks, BLOCK)
    return jnp.where(piece_index >= 0, doc_tokens, -1)


def attend(query_piece, grad_piece, key_buffer, piece_index, block_doc):
    window, _, piece_len, features = key_buffer.shape
    kv_heads = features // HD
    scaling = 1.0 / math.sqrt(HD)
    key_slots = key_buffer[:, 0].reshape(window, piece_len, kv_heads, HD)
    value_slots = key_buffer[:, 1].reshape(window, piece_len, kv_heads, HD)
    keys_flat = key_slots.reshape(window * piece_len, kv_heads, HD)
    values_flat = value_slots.reshape(window * piece_len, kv_heads, HD)
    positions = jnp.arange(piece_len, dtype=jnp.int32)
    query_docs = piece_docs(block_doc, piece_index, piece_len)
    query_pos = piece_index * piece_len + positions
    visible_rows = []
    for slot_index in range(window):
        key_index = piece_index - (window - 1) + slot_index
        key_docs = piece_docs(block_doc, key_index, piece_len)
        key_pos = key_index * piece_len + positions
        visible_rows.append(
            (key_docs[None, :] == query_docs[:, None]) & (key_pos[None, :] <= query_pos[:, None])
        )
    visible = jnp.concatenate(visible_rows, axis=1)

    def key_side(form, left, flat):
        return jnp.einsum(form, left, flat, preferred_element_type=jnp.float32)

    def key_sum(form, weights, flat):
        return jnp.einsum(form, weights, flat, preferred_element_type=jnp.float32)

    def per_key(form, weights, right):
        return jnp.einsum(form, weights, right, preferred_element_type=jnp.float32).reshape(
            window, piece_len, kv_heads, HD
        )

    raw_scores = key_side("qhgd,khd->hgqk", query_piece, keys_flat)
    scores = jnp.where(visible[None, None], raw_scores * scaling, masked_score)
    row_max = jnp.max(scores, axis=-1, keepdims=True)
    log_total = row_max + jnp.log(jnp.sum(jnp.exp(scores - row_max), axis=-1, keepdims=True))
    probs = jnp.exp(scores - log_total)
    probs_low = probs.astype(jnp.bfloat16)
    attended = key_sum("hgqk,khd->qhgd", probs_low, values_flat)
    out_low = attended.astype(jnp.bfloat16)
    out_back = lax.optimization_barrier(out_low).astype(jnp.float32)
    delta = jnp.einsum("qhgd,qhgd->hgq", grad_piece.astype(jnp.float32), out_back)
    dprobs = key_side("qhgd,khd->hgqk", grad_piece, values_flat)
    dscores = (probs * (dprobs - delta[..., None])).astype(jnp.bfloat16)
    query_part = (key_sum("hgqk,khd->qhgd", dscores, keys_flat) * scaling).astype(jnp.bfloat16)
    key_part = per_key("hgqk,qhgd->khd", dscores, query_piece) * scaling
    value_part = per_key("hgqk,qhgd->khd", probs_low, grad_piece)
    grads = jnp.stack(
        [
            key_part.reshape(window, piece_len, features),
            value_part.reshape(window, piece_len, features),
        ],
        axis=1,
    )
    return (out_low.reshape(piece_len, -1), query_part.reshape(piece_len, -1), grads)


def local_wide(queries, keys, values, out_grad, block_doc):
    ctx_size = lax.axis_size("ctx")
    my_index = lax.axis_index("ctx")
    reach_back = min(7, ctx_size // 4 - 1)
    window = reach_back + 1
    levels = window.bit_length() - 1
    piece_len = queries.shape[2]
    kv_heads = keys.shape[3] // HD
    group = HQ // HK
    query_all = queries[:, 0].reshape(2, piece_len, kv_heads, group, HD)
    grad_all = out_grad[:, 0].reshape(2, piece_len, kv_heads, group, HD)
    paired = jnp.stack([keys[:, 0], values[:, 0]], axis=1)
    low_buffer = paired[0][None]
    high_buffer = paired[1][None]
    for level_bit in range(levels):
        distance = 1 << level_bit
        low_buffer = jnp.concatenate([move_keys(low_buffer, distance), low_buffer], axis=0)
        high_buffer = jnp.concatenate([move_keys(high_buffer, -distance), high_buffer], axis=0)
    high_index = 2 * ctx_size - 1 - my_index
    low_out, low_qgrad, low_grads = attend(
        query_all[0], grad_all[0], low_buffer, my_index, block_doc
    )
    high_out, high_qgrad, high_grads = attend(
        query_all[1], grad_all[1], high_buffer, high_index, block_doc
    )
    low_back = low_grads
    high_back = high_grads
    for level_bit in reversed(range(levels)):
        distance = 1 << level_bit
        low_back = low_back[distance:] + move_grads(low_back[:distance], -distance)
        high_back = high_back[distance:] + move_grads(high_back[:distance], distance)
    low_total = low_back[0]
    high_total = high_back[0]
    attn_pair = jnp.stack([low_out, high_out])[:, None]
    qgrad_pair = jnp.stack([low_qgrad, high_qgrad])[:, None]
    key_pair = jnp.stack([low_total[0], high_total[0]]).astype(jnp.bfloat16)[:, None]
    value_pair = jnp.stack([low_total[1], high_total[1]]).astype(jnp.bfloat16)[:, None]
    return (attn_pair, qgrad_pair, key_pair, value_pair)


GROUP = HQ // HK
CHUNK = 2 * HD
LOG2_SCALE = math.log2(math.e) / math.sqrt(HD)
SCALE = 1.0 / math.sqrt(HD)
VMEM_LIMIT = 24 * 1024 * 1024

F32 = jnp.float32
BF16 = jnp.bfloat16

in_vmem = pl.BlockSpec(memory_space=pltpu.VMEM)
in_hbm = pl.BlockSpec(memory_space=pltpu.HBM)
in_smem = pl.BlockSpec(memory_space=pltpu.SMEM)


def dot(left, right):
    return jnp.dot(left, right, preferred_element_type=F32)


def dot_t(left, right):
    return lax.dot_general(left, right, (((1,), (1,)), ((), ())), preferred_element_type=F32)


def near_slot():
    return lax.rem(lax.axis_index("ctx"), 2)


def far_slot():
    return 1 - near_slot()


def linked(doc_ref, slot):
    pairs = lax.axis_size("ctx")
    me = lax.axis_index("ctx")
    piece = jnp.where(slot == 0, me, 2 * pairs - 1 - me)
    same = doc_ref[piece] == doc_ref[jnp.maximum(piece - 1, 0)]
    return jnp.where(jnp.logical_and(piece > 0, same), 0.0, masked_score).astype(F32)


def lanes(ref, first, count):
    parts = [ref[:, pl.ds(first + i * HD, HD)] for i in range(count)]
    return jnp.concatenate(parts, axis=0)


def causal(rows, columns):
    key = lax.broadcasted_iota(jnp.int32, (rows, columns), 0)
    query = lax.broadcasted_iota(jnp.int32, (rows, columns), 1)
    return key <= lax.rem(query, rows)


def fetch_pairs(pairs_of_refs, sems):
    copies = [pltpu.make_async_copy(a, b, sems.at[i]) for i, (a, b) in enumerate(pairs_of_refs)]
    for copy in copies:
        copy.start()
    return copies


def pick_kernel(needed, keys, values, block_doc, far_kv, near_kv, case, doc, sems):
    far, near = far_slot(), near_slot()
    copies = fetch_pairs(
        [
            (block_doc, doc),
            (keys.at[far, 0], far_kv.at[0]),
            (values.at[far, 0], far_kv.at[1]),
            (keys.at[near, 0], near_kv.at[0]),
            (values.at[near, 0], near_kv.at[1]),
        ],
        sems,
    )
    copies[0].wait()
    case[0] = needed(doc)
    for copy in copies[1:]:
        copy.wait()


def pick(keys, values, block_doc, needed):
    _, _, piece_len, features = keys.shape
    shape = pltpu.VMEM((2, piece_len, features), BF16)
    return pl.pallas_call(
        functools.partial(pick_kernel, needed),
        out_shape=(
            shape,
            shape,
            pltpu.SMEM((1,), jnp.int32),
            pltpu.SMEM(block_doc.shape, jnp.int32),
        ),
        in_specs=[in_hbm, in_hbm, in_hbm],
        out_specs=(in_vmem, in_vmem, in_smem, in_smem),
        scratch_shapes=[pltpu.SemaphoreType.DMA((5,))],
        name="pick",
    )(keys, values, block_doc)


def keep_kernel(*refs):
    pass


def keep(far_kv, near_kv):
    shape = pltpu.VMEM(far_kv.shape, BF16)
    return pl.pallas_call(
        keep_kernel,
        out_shape=(shape, shape),
        in_specs=[in_vmem, in_vmem],
        out_specs=(in_vmem, in_vmem),
        input_output_aliases={0: 0, 1: 1},
        cost_estimate=pl.CostEstimate(flops=10**10, bytes_accessed=10**6, transcendentals=0),
        compiler_params=pltpu.CompilerParams(vmem_limit_bytes=VMEM_LIMIT),
        name="keep",
    )(far_kv, near_kv)


def diagonal_kernel(doc, kv, queries, out_grad, weights, dprobs, stats):
    near = near_slot()
    q, do = queries.at[near, 0], out_grad.at[near, 0]
    kv_heads = kv.shape[2] // HD
    bias = linked(doc, near)
    bias_far = linked(doc, 1 - near)
    mask = causal(kv.shape[1], CHUNK)
    for j in range(kv_heads):
        k = kv[0, :, pl.ds(j * HD, HD)]
        v = kv[1, :, pl.ds(j * HD, HD)]
        for h in range(0, GROUP, 2):
            first = (j * GROUP + h) * HD
            at = pl.ds(first, CHUNK)
            logits = jnp.where(mask, dot_t(k, lanes(q, first, 2)) * LOG2_SCALE, masked_score)
            top = jnp.max(logits, axis=0, keepdims=True)
            e = jnp.exp2(logits - top)
            dp = dot_t(v, lanes(do, first, 2))
            weights[:, at] = e
            dprobs[:, at] = dp
            stats[0:1, at] = top
            stats[1:2, at] = jnp.sum(e, axis=0, keepdims=True)
            stats[2:3, at] = jnp.sum(e * dp, axis=0, keepdims=True)
            stats[3:4, at] = jnp.full((1, CHUNK), bias, F32)
            stats[4:5, at] = jnp.full((1, CHUNK), bias_far, F32)


def diagonal(block_doc, kv, queries, out_grad):
    _, _, piece_len, width = queries.shape
    return pl.pallas_call(
        diagonal_kernel,
        out_shape=(
            pltpu.VMEM((piece_len, width), F32),
            pltpu.VMEM((piece_len, width), F32),
            pltpu.VMEM((8, width), F32),
        ),
        in_specs=[in_smem, in_vmem, in_vmem, in_vmem],
        out_specs=(in_vmem,) * 3,
        compiler_params=pltpu.CompilerParams(vmem_limit_bytes=VMEM_LIMIT),
        name="diagonal",
    )(block_doc, kv, queries, out_grad)


def whole_kernel(stats, kv, kv_before, queries, out_grad, before, own, p, ds):
    far = far_slot()
    q, do = queries.at[far, 0], out_grad.at[far, 0]
    kv_heads = kv.shape[2] // HD
    piece_len = kv.shape[1]
    bias = stats[4:5, :CHUNK]
    mask = causal(piece_len, CHUNK)
    for j in range(kv_heads):
        head = pl.ds(j * HD, HD)
        k = jnp.concatenate([kv_before[0, :, head], kv[0, :, head]], axis=0)
        v = jnp.concatenate([kv_before[1, :, head], kv[1, :, head]], axis=0)
        for h in range(0, GROUP, 2):
            first = (j * GROUP + h) * HD
            at = pl.ds(first, CHUNK)
            logits = dot_t(k, lanes(q, first, 2)) * LOG2_SCALE
            cross = logits[:piece_len]
            here = jnp.where(mask, logits[piece_len:], masked_score)
            top = jnp.maximum(
                jnp.max(cross, axis=0, keepdims=True) + bias, jnp.max(here, axis=0, keepdims=True)
            )
            e = jnp.concatenate([jnp.exp2(cross - (top - bias)), jnp.exp2(here - top)], axis=0)
            dp = dot_t(v, lanes(do, first, 2))
            ratio = 1.0 / jnp.sum(e, axis=0, keepdims=True)
            delta = jnp.sum(e * dp, axis=0, keepdims=True) * ratio
            prob = e * ratio
            p[:, at] = prob.astype(BF16)
            ds[:, at] = (prob * (dp - delta)).astype(BF16)
        cols = pl.ds(j * GROUP * HD, GROUP * HD)
        dk = dot(ds[:, cols], lanes(q, j * GROUP * HD, GROUP)) * SCALE
        dv = dot(p[:, cols], lanes(do, j * GROUP * HD, GROUP))
        before[0, :, head] = dk[:piece_len].astype(BF16)
        before[1, :, head] = dv[:piece_len].astype(BF16)
        own[0, :, head] = dk[piece_len:]
        own[1, :, head] = dv[piece_len:]


def whole(stats, kv, kv_before, queries, out_grad):
    _, piece_len, features = kv.shape
    width = queries.shape[3]
    return pl.pallas_call(
        whole_kernel,
        out_shape=(
            pltpu.VMEM((2, piece_len, features), BF16),
            pltpu.VMEM((2, piece_len, features), F32),
            pltpu.VMEM((2 * piece_len, width), BF16),
            pltpu.VMEM((2 * piece_len, width), BF16),
        ),
        in_specs=[in_vmem] * 5,
        out_specs=(in_vmem,) * 4,
        compiler_params=pltpu.CompilerParams(vmem_limit_bytes=VMEM_LIMIT),
        name="whole",
    )(stats, kv, kv_before, queries, out_grad)


def cross_kernel(doc, kv_before, queries, out_grad, stats, behind, before, p, ds, after):
    near = near_slot()
    q, do = queries.at[near, 0], out_grad.at[near, 0]
    piece_len, features = kv_before.shape[1:]
    seen = linked(doc, near) == 0.0

    @pl.when(seen)
    def _():
        for j in range(features // HD):
            head = pl.ds(j * HD, HD)
            k = kv_before[0, :, head]
            v = kv_before[1, :, head]
            for h in range(0, GROUP, 2):
                first = (j * GROUP + h) * HD
                at = pl.ds(first, CHUNK)
                top_here, total_here, dot_here = (stats[i : i + 1, at] for i in range(3))
                logits = dot_t(k, lanes(q, first, 2)) * LOG2_SCALE
                top = jnp.maximum(jnp.max(logits, axis=0, keepdims=True), top_here)
                e = jnp.exp2(logits - top)
                dp = dot_t(v, lanes(do, first, 2))
                shrink = jnp.exp2(top_here - top)
                ratio = 1.0 / (total_here * shrink + jnp.sum(e, axis=0, keepdims=True))
                delta = (dot_here * shrink + jnp.sum(e * dp, axis=0, keepdims=True)) * ratio
                prob = e * ratio
                p[:, at] = prob.astype(BF16)
                ds[:, at] = (prob * (dp - delta)).astype(BF16)
                after[0:1, at] = shrink * ratio
                after[1:2, at] = delta
            cols = pl.ds(j * GROUP * HD, GROUP * HD)
            dk = dot(ds[:, cols], lanes(q, j * GROUP * HD, GROUP)) * SCALE
            dv = dot(p[:, cols], lanes(do, j * GROUP * HD, GROUP))
            before[0, :, head] = dk.astype(BF16)
            before[1, :, head] = dv.astype(BF16)

    @pl.when(jnp.logical_not(seen))
    def _():
        before[...] = jnp.zeros_like(before)
        p[...] = jnp.zeros_like(p)
        ds[...] = jnp.zeros_like(ds)
        ratio = 1.0 / stats[1:2, :]
        after[0:1, :] = ratio
        after[1:2, :] = stats[2:3, :] * ratio


def cross(doc, kv_before, queries, out_grad, stats, behind):
    _, piece_len, features = kv_before.shape
    width = queries.shape[3]
    return pl.pallas_call(
        cross_kernel,
        out_shape=(
            pltpu.VMEM((2, piece_len, features), BF16),
            pltpu.VMEM((piece_len, width), BF16),
            pltpu.VMEM((piece_len, width), BF16),
            pltpu.VMEM((8, width), F32),
        ),
        in_specs=[in_smem] + [in_vmem] * 5,
        out_specs=(in_vmem,) * 4,
        compiler_params=pltpu.CompilerParams(vmem_limit_bytes=VMEM_LIMIT),
        name="cross",
    )(doc, kv_before, queries, out_grad, stats, behind)


def turn(wide, ref, first):
    for i in range(wide.shape[1] // HD):
        ref[:, pl.ds(first + i * HD, HD)] = wide[:, i * HD : (i + 1) * HD].T


def rest_kernel(alone, *refs):
    near_kv, queries, out_grad, weights, dprobs, after, far_kv, mate_kv, p_far, ds_far = refs[:10]
    if not alone:
        next_kv, p_next, ds_next = refs[10:13]
    out, q_grad, own, o, dq, p, ds, sems = refs[-8:]
    near, far = near_slot(), far_slot()
    q, do = queries.at[near, 0], out_grad.at[near, 0]
    kv_heads = near_kv.shape[2] // HD
    span = GROUP * HD
    backs = []

    def give_back(side, slot, j):
        cols = pl.ds(j * span, span)
        for n, (a, b) in enumerate(((o, out), (dq, q_grad))):
            sem = sems.at[(side * kv_heads + j) * 2 + n]
            back = pltpu.make_async_copy(a.at[side, :, cols], b.at[slot, 0, :, cols], sem)
            back.start()
            backs.append(back)

    for j in range(kv_heads):
        head = pl.ds(j * HD, HD)
        k_t = jnp.concatenate([mate_kv[0, :, head], far_kv[0, :, head]], axis=0).T
        v_t = jnp.concatenate([mate_kv[1, :, head], far_kv[1, :, head]], axis=0).T
        for h in range(0, GROUP, 2):
            first = (j * GROUP + h) * HD
            at = pl.ds(first, CHUNK)
            turn(dot(v_t, p_far[:, at]).astype(BF16), o.at[1], first)
            turn((dot(k_t, ds_far[:, at]) * SCALE).astype(BF16), dq.at[1], first)
        give_back(1, far, j)
    for j in range(kv_heads):
        head = pl.ds(j * HD, HD)
        if alone:
            k_t, v_t = near_kv[0, :, head].T, near_kv[1, :, head].T
        else:
            k_t = jnp.concatenate([next_kv[0, :, head], near_kv[0, :, head]], axis=0).T
            v_t = jnp.concatenate([next_kv[1, :, head], near_kv[1, :, head]], axis=0).T
        for h in range(0, GROUP, 2):
            first = (j * GROUP + h) * HD
            at = pl.ds(first, CHUNK)
            if alone:
                ratio = 1.0 / after[1:2, at]
                delta = after[2:3, at] * ratio
            else:
                ratio, delta = after[0:1, at], after[1:2, at]
            prob = weights[:, at] * ratio
            prob_low = prob.astype(BF16)
            ds_low = (prob * (dprobs[:, at] - delta)).astype(BF16)
            p[:, pl.ds(h * HD, CHUNK)] = prob_low
            ds[:, pl.ds(h * HD, CHUNK)] = ds_low
            if not alone:
                prob_low = jnp.concatenate([p_next[:, at], prob_low], axis=0)
                ds_low = jnp.concatenate([ds_next[:, at], ds_low], axis=0)
            turn(dot(v_t, prob_low).astype(BF16), o.at[0], first)
            turn((dot(k_t, ds_low) * SCALE).astype(BF16), dq.at[0], first)
        give_back(0, near, j)
        own[0, :, head] = dot(ds[...], lanes(q, j * span, GROUP)) * SCALE
        own[1, :, head] = dot(p[...], lanes(do, j * span, GROUP))
    for back in backs:
        back.wait()


def rest(alone, *operands, shape):
    _, piece_len, features = operands[0].shape
    width = shape[3]
    kv_heads = features // HD
    wide = pltpu.HBM(shape, BF16)
    return pl.pallas_call(
        functools.partial(rest_kernel, alone),
        out_shape=(wide, wide, pltpu.VMEM((2, piece_len, features), F32)),
        in_specs=[in_vmem] * len(operands),
        out_specs=(in_hbm, in_hbm, in_vmem),
        scratch_shapes=[pltpu.VMEM((2, piece_len, width), BF16)] * 2
        + [pltpu.VMEM((piece_len, GROUP * HD), BF16)] * 2
        + [pltpu.SemaphoreType.DMA((4 * kv_heads,))],
        compiler_params=pltpu.CompilerParams(vmem_limit_bytes=VMEM_LIMIT),
        name="rest",
    )(*operands)


def total_kernel(near_own, far_own, near_back, *refs):
    k_grad, v_grad, k_low, v_low, sems = refs[-5:]
    near, far = near_slot(), far_slot()
    for n, low in enumerate((k_low, v_low)):
        low[near, 0] = (near_own[n] + near_back[n].astype(F32)).astype(BF16)
        mine = far_own[n]
        if len(refs) > 5:
            mine = mine + refs[0][n].astype(F32)
        low[far, 0] = mine.astype(BF16)
    for copy in fetch_pairs([(k_low, k_grad), (v_low, v_grad)], sems):
        copy.wait()


def total(*operands):
    _, piece_len, features = operands[0].shape
    shape = (2, 1, piece_len, features)
    return pl.pallas_call(
        total_kernel,
        out_shape=(pltpu.HBM(shape, BF16),) * 2,
        in_specs=[in_vmem] * len(operands),
        out_specs=(in_hbm,) * 2,
        scratch_shapes=[pltpu.VMEM(shape, BF16)] * 2 + [pltpu.SemaphoreType.DMA((2,))],
        compiler_params=pltpu.CompilerParams(vmem_limit_bytes=VMEM_LIMIT),
        name="total",
    )(*operands)


def far_links(pairs):
    low = [(i, i + 1, i) for i in range(3, pairs - 1, 2)]
    high = [(i + 1, i, 2 * pairs - 2 - i) for i in range(1, pairs - 3, 2)]
    return low + high


def hops(flow):
    (y, x, core), (to_y, to_x, to_core) = ((i // 4, i // 2 % 2, i % 2) for i in flow)
    steps = []
    if x != to_x:
        steps.append(("x", to_x, y))
    if y != to_y:
        steps.append(("y", to_y, to_x))
    return steps, core != to_core


def burden(flow, taken, late):
    steps, other_core = hops(flow)
    weight = 0.1
    if steps:
        weight = len(steps) + 0.3 * other_core + (1.5 if flow[1] == 0 else 0.5 * (flow[1] % 2))
        weight += 3.0 * sum(step in taken for step in steps)
        weight += 0.7 * (flow[1] in late)
    return weight


SPARE = {
    ((5, 6), (2, 1)): [(3, 2), (4, 5), (6, 7), (1, 0), (0, 3), (7, 4)],
    ((6, 5), (1, 2)): [(2, 3), (5, 4), (7, 6), (0, 1), (3, 0), (4, 7)],
}


def complete(route, pairs):
    if pairs == 8 and tuple(route) in SPARE:
        return route + SPARE[tuple(route)]
    sources = [i for i in range(pairs) if i not in {a for a, _ in route}]
    targets = [i for i in range(pairs) if i not in {b for _, b in route}]
    if pairs == 8:
        taken = {step for flow in route for step in hops(flow)[0]}
        late = {i for flow in route for i in flow}
        found = [(math.inf, [])]

        def search(rest_of, free, cost, chosen):
            if cost >= found[0][0]:
                return
            if not rest_of:
                found[0] = (cost, chosen)
                return
            for b in free:
                flow = (rest_of[0], b)
                if flow[0] != b:
                    left = [t for t in free if t != b]
                    more = burden(flow, taken, late)
                    search(rest_of[1:], left, cost + more, chosen + [flow])

        search(sources, targets, 0.0, [])
        if found[0][0] < math.inf:
            return route + found[0][1]
    for turn_by in range(len(targets)):
        turned = targets[turn_by:] + targets[:turn_by]
        if all(a != b for a, b in zip(sources, turned)):
            return route + list(zip(sources, turned))
    return route


def attend_pairs(links, queries, out_grad, doc, far_kv, near_kv):
    pairs = lax.axis_size("ctx")
    mates = [(i, i ^ 1) for i in range(pairs) if i ^ 1 < pairs]
    flows = [(a, b) for a, b, _ in links]
    far_kv, near_kv = keep(far_kv, near_kv)
    mate_kv = lax.ppermute(near_kv, "ctx", mates)
    if links:
        next_kv = lax.ppermute(far_kv, "ctx", complete(flows, pairs))
    weights, dprobs, stats = diagonal(doc, near_kv, queries, out_grad)
    mate_grads, far_own, p_far, ds_far = whole(stats, far_kv, mate_kv, queries, out_grad)
    mate_back = lax.ppermute(mate_grads, "ctx", mates)
    after, more, far_back = stats, (), ()
    if links:
        next_grads, p_next, ds_next, after = cross(
            doc, next_kv, queries, out_grad, stats, mate_grads
        )
        more = (next_kv, p_next, ds_next)
        back = [(b, a) for a, b in flows]
        far_back = (lax.ppermute(next_grads, "ctx", complete(back, pairs)),)
    out, q_grad, near_own = rest(
        not links, near_kv, queries, out_grad, weights, dprobs, after, far_kv, mate_kv, p_far,
        ds_far, *more, shape=queries.shape,
    )
    k_grad, v_grad = total(near_own, far_own, mate_back, *far_back)
    return (out, q_grad, k_grad, v_grad)


def local_pairs(queries, keys, values, out_grad, block_doc):
    links = far_links(lax.axis_size("ctx"))
    low = [link for link in links if link[0] < link[1]]
    high = [link for link in links if link[0] > link[1]]
    outer = [link for link in links if min(link[:2]) % 4 == 3]
    inner = [link for link in links if min(link[:2]) % 4 == 1]

    def needed(doc):
        def linked_among(*groups):
            some = [link for link in links if all(link in group for group in groups)]
            same = [doc[first] == doc[first + 1] for _, _, first in some]
            return functools.reduce(jnp.logical_or, same)

        any_outer = linked_among(outer)
        any_low, any_high = linked_among(low), linked_among(high)
        side = jnp.where(any_low, jnp.where(any_high, 4, 2), 3)
        near_only = jnp.where(linked_among(inner), 1, 0)
        return jnp.where(any_outer, side, near_only)

    far_kv, near_kv, case, doc = pick(keys, values, block_doc, needed)
    branches = [functools.partial(attend_pairs, some) for some in ([], inner, low, high, links)]
    return lax.switch(case[0], branches, queries, out_grad, doc, far_kv, near_kv)


def local(queries, keys, values, out_grad, block_doc):
    window = min(7, lax.axis_size("ctx") // 4 - 1) + 1
    piece_len = queries.shape[2]
    even = lax.axis_size("ctx") % 2 == 0
    if window == 2 and piece_len == BLOCK and even:
        return local_pairs(queries, keys, values, out_grad, block_doc)
    return local_wide(queries, keys, values, out_grad, block_doc)


def solution(mesh):
    in_specs = (
        P(None, "ctx", None, "tp"),
        P(None, "ctx", None, "tp"),
        P(None, "ctx", None, "tp"),
        P(None, "ctx", None, "tp"),
        P(),
    )
    out_specs = (
        P(None, "ctx", None, "tp"),
        P(None, "ctx", None, "tp"),
        P(None, "ctx", None, "tp"),
        P(None, "ctx", None, "tp"),
    )
    return jax.shard_map(local, mesh=mesh, in_specs=in_specs, out_specs=out_specs, check_vma=False)
```

```python
import functools
import math

import jax
import jax.numpy as jnp
from jax import lax
from jax.experimental import pallas as pl
from jax.experimental.pallas import tpu as pltpu
from jax.sharding import PartitionSpec as P

HQ = 64
HK = 8
HD = 128
BLOCK = 128


masked_score = -1e30


def shifted(block, axis, distance):
    devices = range(lax.axis_size(axis))
    route = [(i - distance, i) for i in devices if i - distance in devices]
    return lax.ppermute(block, axis, route)


def move_keys(payload, distance):
    return shifted(payload, "ctx", distance)


def move_grads(payload, distance):
    return shifted(payload.astype(jnp.bfloat16), "ctx", distance).astype(payload.dtype)


def piece_docs(block_doc, piece_index, piece_len):
    per_piece = piece_len // BLOCK
    start = jnp.maximum(piece_index, 0) * per_piece
    doc_blocks = lax.dynamic_slice_in_dim(block_doc, start, per_piece, 0)
    doc_tokens = jnp.repeat(doc_blocks, BLOCK)
    return jnp.where(piece_index >= 0, doc_tokens, -1)


def attend(query_piece, grad_piece, key_buffer, piece_index, block_doc):
    window, _, piece_len, features = key_buffer.shape
    kv_heads = features // HD
    scaling = 1.0 / math.sqrt(HD)
    key_slots = key_buffer[:, 0].reshape(window, piece_len, kv_heads, HD)
    value_slots = key_buffer[:, 1].reshape(window, piece_len, kv_heads, HD)
    keys_flat = key_slots.reshape(window * piece_len, kv_heads, HD)
    values_flat = value_slots.reshape(window * piece_len, kv_heads, HD)
    positions = jnp.arange(piece_len, dtype=jnp.int32)
    query_docs = piece_docs(block_doc, piece_index, piece_len)
    query_pos = piece_index * piece_len + positions
    visible_rows = []
    for slot_index in range(window):
        key_index = piece_index - (window - 1) + slot_index
        key_docs = piece_docs(block_doc, key_index, piece_len)
        key_pos = key_index * piece_len + positions
        visible_rows.append(
            (key_docs[None, :] == query_docs[:, None]) & (key_pos[None, :] <= query_pos[:, None])
        )
    visible = jnp.concatenate(visible_rows, axis=1)

    def key_side(form, left, flat):
        return jnp.einsum(form, left, flat, preferred_element_type=jnp.float32)

    def key_sum(form, weights, flat):
        return jnp.einsum(form, weights, flat, preferred_element_type=jnp.float32)

    def per_key(form, weights, right):
        return jnp.einsum(form, weights, right, preferred_element_type=jnp.float32).reshape(
            window, piece_len, kv_heads, HD
        )

    raw_scores = key_side("qhgd,khd->hgqk", query_piece, keys_flat)
    scores = jnp.where(visible[None, None], raw_scores * scaling, masked_score)
    row_max = jnp.max(scores, axis=-1, keepdims=True)
    log_total = row_max + jnp.log(jnp.sum(jnp.exp(scores - row_max), axis=-1, keepdims=True))
    probs = jnp.exp(scores - log_total)
    probs_low = probs.astype(jnp.bfloat16)
    attended = key_sum("hgqk,khd->qhgd", probs_low, values_flat)
    out_low = attended.astype(jnp.bfloat16)
    out_back = lax.optimization_barrier(out_low).astype(jnp.float32)
    delta = jnp.einsum("qhgd,qhgd->hgq", grad_piece.astype(jnp.float32), out_back)
    dprobs = key_side("qhgd,khd->hgqk", grad_piece, values_flat)
    dscores = (probs * (dprobs - delta[..., None])).astype(jnp.bfloat16)
    query_part = (key_sum("hgqk,khd->qhgd", dscores, keys_flat) * scaling).astype(jnp.bfloat16)
    key_part = per_key("hgqk,qhgd->khd", dscores, query_piece) * scaling
    value_part = per_key("hgqk,qhgd->khd", probs_low, grad_piece)
    grads = jnp.stack(
        [
            key_part.reshape(window, piece_len, features),
            value_part.reshape(window, piece_len, features),
        ],
        axis=1,
    )
    return (out_low.reshape(piece_len, -1), query_part.reshape(piece_len, -1), grads)


def local_wide(queries, keys, values, out_grad, block_doc):
    ctx_size = lax.axis_size("ctx")
    my_index = lax.axis_index("ctx")
    reach_back = min(7, ctx_size // 4 - 1)
    window = reach_back + 1
    levels = window.bit_length() - 1
    piece_len = queries.shape[2]
    kv_heads = keys.shape[3] // HD
    group = HQ // HK
    query_all = queries[:, 0].reshape(2, piece_len, kv_heads, group, HD)
    grad_all = out_grad[:, 0].reshape(2, piece_len, kv_heads, group, HD)
    paired = jnp.stack([keys[:, 0], values[:, 0]], axis=1)
    low_buffer = paired[0][None]
    high_buffer = paired[1][None]
    for level_bit in range(levels):
        distance = 1 << level_bit
        low_buffer = jnp.concatenate([move_keys(low_buffer, distance), low_buffer], axis=0)
        high_buffer = jnp.concatenate([move_keys(high_buffer, -distance), high_buffer], axis=0)
    high_index = 2 * ctx_size - 1 - my_index
    low_out, low_qgrad, low_grads = attend(
        query_all[0], grad_all[0], low_buffer, my_index, block_doc
    )
    high_out, high_qgrad, high_grads = attend(
        query_all[1], grad_all[1], high_buffer, high_index, block_doc
    )
    low_back = low_grads
    high_back = high_grads
    for level_bit in reversed(range(levels)):
        distance = 1 << level_bit
        low_back = low_back[distance:] + move_grads(low_back[:distance], -distance)
        high_back = high_back[distance:] + move_grads(high_back[:distance], distance)
    low_total = low_back[0]
    high_total = high_back[0]
    attn_pair = jnp.stack([low_out, high_out])[:, None]
    qgrad_pair = jnp.stack([low_qgrad, high_qgrad])[:, None]
    key_pair = jnp.stack([low_total[0], high_total[0]]).astype(jnp.bfloat16)[:, None]
    value_pair = jnp.stack([low_total[1], high_total[1]]).astype(jnp.bfloat16)[:, None]
    return (attn_pair, qgrad_pair, key_pair, value_pair)


GROUP = HQ // HK
CHUNK = 2 * HD
LOG2_SCALE = math.log2(math.e) / math.sqrt(HD)
SCALE = 1.0 / math.sqrt(HD)
VMEM_LIMIT = 24 * 1024 * 1024

F32 = jnp.float32
BF16 = jnp.bfloat16

in_vmem = pl.BlockSpec(memory_space=pltpu.VMEM)
in_hbm = pl.BlockSpec(memory_space=pltpu.HBM)
in_smem = pl.BlockSpec(memory_space=pltpu.SMEM)


def dot(left, right):
    return jnp.dot(left, right, preferred_element_type=F32)


def dot_t(left, right):
    return lax.dot_general(left, right, (((1,), (1,)), ((), ())), preferred_element_type=F32)


def near_slot():
    return lax.rem(lax.axis_index("ctx"), 2)


def far_slot():
    return 1 - near_slot()


def linked(doc_ref, slot):
    pairs = lax.axis_size("ctx")
    me = lax.axis_index("ctx")
    piece = jnp.where(slot == 0, me, 2 * pairs - 1 - me)
    same = doc_ref[piece] == doc_ref[jnp.maximum(piece - 1, 0)]
    return jnp.where(jnp.logical_and(piece > 0, same), 0.0, masked_score).astype(F32)


def lanes(ref, first, count):
    parts = [ref[:, pl.ds(first + i * HD, HD)] for i in range(count)]
    return jnp.concatenate(parts, axis=0)


def causal(rows, columns):
    key = lax.broadcasted_iota(jnp.int32, (rows, columns), 0)
    query = lax.broadcasted_iota(jnp.int32, (rows, columns), 1)
    return key <= lax.rem(query, rows)


def fetch_pairs(pairs_of_refs, sems):
    copies = [pltpu.make_async_copy(a, b, sems.at[i]) for i, (a, b) in enumerate(pairs_of_refs)]
    for copy in copies:
        copy.start()
    return copies


def pick_kernel(needed, keys, values, block_doc, far_kv, near_kv, case, doc, sems):
    far, near = far_slot(), near_slot()
    copies = fetch_pairs(
        [
            (block_doc, doc),
            (keys.at[far, 0], far_kv.at[0]),
            (values.at[far, 0], far_kv.at[1]),
            (keys.at[near, 0], near_kv.at[0]),
            (values.at[near, 0], near_kv.at[1]),
        ],
        sems,
    )
    copies[0].wait()
    case[0] = needed(doc)
    for copy in copies[1:]:
        copy.wait()


def pick(keys, values, block_doc, needed):
    _, _, piece_len, features = keys.shape
    shape = pltpu.VMEM((2, piece_len, features), BF16)
    return pl.pallas_call(
        functools.partial(pick_kernel, needed),
        out_shape=(
            shape,
            shape,
            pltpu.SMEM((1,), jnp.int32),
            pltpu.SMEM(block_doc.shape, jnp.int32),
        ),
        in_specs=[in_hbm, in_hbm, in_hbm],
        out_specs=(in_vmem, in_vmem, in_smem, in_smem),
        scratch_shapes=[pltpu.SemaphoreType.DMA((5,))],
        name="pick",
    )(keys, values, block_doc)


def keep_kernel(*refs):
    pass


def keep(far_kv, near_kv):
    shape = pltpu.VMEM(far_kv.shape, BF16)
    return pl.pallas_call(
        keep_kernel,
        out_shape=(shape, shape),
        in_specs=[in_vmem, in_vmem],
        out_specs=(in_vmem, in_vmem),
        input_output_aliases={0: 0, 1: 1},
        cost_estimate=pl.CostEstimate(flops=10**10, bytes_accessed=10**6, transcendentals=0),
        compiler_params=pltpu.CompilerParams(vmem_limit_bytes=VMEM_LIMIT),
        name="keep",
    )(far_kv, near_kv)


def diagonal_kernel(doc, kv, queries, out_grad, weights, dprobs, stats):
    near = near_slot()
    q, do = queries.at[near, 0], out_grad.at[near, 0]
    kv_heads = kv.shape[2] // HD
    bias = linked(doc, near)
    bias_far = linked(doc, 1 - near)
    mask = causal(kv.shape[1], CHUNK)
    for j in range(kv_heads):
        k = kv[0, :, pl.ds(j * HD, HD)]
        v = kv[1, :, pl.ds(j * HD, HD)]
        for h in range(0, GROUP, 2):
            first = (j * GROUP + h) * HD
            at = pl.ds(first, CHUNK)
            logits = jnp.where(mask, dot_t(k, lanes(q, first, 2)) * LOG2_SCALE, masked_score)
            top = jnp.max(logits, axis=0, keepdims=True)
            e = jnp.exp2(logits - top)
            dp = dot_t(v, lanes(do, first, 2))
            weights[:, at] = e
            dprobs[:, at] = dp
            stats[0:1, at] = top
            stats[1:2, at] = jnp.sum(e, axis=0, keepdims=True)
            stats[2:3, at] = jnp.sum(e * dp, axis=0, keepdims=True)
            stats[3:4, at] = jnp.full((1, CHUNK), bias, F32)
            stats[4:5, at] = jnp.full((1, CHUNK), bias_far, F32)


def diagonal(block_doc, kv, queries, out_grad):
    _, _, piece_len, width = queries.shape
    return pl.pallas_call(
        diagonal_kernel,
        out_shape=(
            pltpu.VMEM((piece_len, width), F32),
            pltpu.VMEM((piece_len, width), F32),
            pltpu.VMEM((8, width), F32),
        ),
        in_specs=[in_smem, in_vmem, in_vmem, in_vmem],
        out_specs=(in_vmem,) * 3,
        compiler_params=pltpu.CompilerParams(vmem_limit_bytes=VMEM_LIMIT),
        name="diagonal",
    )(block_doc, kv, queries, out_grad)


def whole_kernel(stats, kv, kv_before, queries, out_grad, before, own, p, ds):
    far = far_slot()
    q, do = queries.at[far, 0], out_grad.at[far, 0]
    kv_heads = kv.shape[2] // HD
    piece_len = kv.shape[1]
    bias = stats[4:5, :CHUNK]
    mask = causal(piece_len, CHUNK)
    for j in range(kv_heads):
        head = pl.ds(j * HD, HD)
        k = jnp.concatenate([kv_before[0, :, head], kv[0, :, head]], axis=0)
        v = jnp.concatenate([kv_before[1, :, head], kv[1, :, head]], axis=0)
        for h in range(0, GROUP, 2):
            first = (j * GROUP + h) * HD
            at = pl.ds(first, CHUNK)
            logits = dot_t(k, lanes(q, first, 2)) * LOG2_SCALE
            cross = logits[:piece_len]
            here = jnp.where(mask, logits[piece_len:], masked_score)
            top = jnp.maximum(
                jnp.max(cross, axis=0, keepdims=True) + bias, jnp.max(here, axis=0, keepdims=True)
            )
            e = jnp.concatenate([jnp.exp2(cross - (top - bias)), jnp.exp2(here - top)], axis=0)
            dp = dot_t(v, lanes(do, first, 2))
            ratio = 1.0 / jnp.sum(e, axis=0, keepdims=True)
            delta = jnp.sum(e * dp, axis=0, keepdims=True) * ratio
            prob = e * ratio
            p[:, at] = prob.astype(BF16)
            ds[:, at] = (prob * (dp - delta)).astype(BF16)
        cols = pl.ds(j * GROUP * HD, GROUP * HD)
        dk = dot(ds[:, cols], lanes(q, j * GROUP * HD, GROUP)) * SCALE
        dv = dot(p[:, cols], lanes(do, j * GROUP * HD, GROUP))
        before[0, :, head] = dk[:piece_len].astype(BF16)
        before[1, :, head] = dv[:piece_len].astype(BF16)
        own[0, :, head] = dk[piece_len:]
        own[1, :, head] = dv[piece_len:]


def whole(stats, kv, kv_before, queries, out_grad):
    _, piece_len, features = kv.shape
    width = queries.shape[3]
    return pl.pallas_call(
        whole_kernel,
        out_shape=(
            pltpu.VMEM((2, piece_len, features), BF16),
            pltpu.VMEM((2, piece_len, features), F32),
            pltpu.VMEM((2 * piece_len, width), BF16),
            pltpu.VMEM((2 * piece_len, width), BF16),
        ),
        in_specs=[in_vmem] * 5,
        out_specs=(in_vmem,) * 4,
        compiler_params=pltpu.CompilerParams(vmem_limit_bytes=VMEM_LIMIT),
        name="whole",
    )(stats, kv, kv_before, queries, out_grad)


def cross_kernel(doc, kv_before, queries, out_grad, stats, behind, before, p, ds, after):
    near = near_slot()
    q, do = queries.at[near, 0], out_grad.at[near, 0]
    piece_len, features = kv_before.shape[1:]
    seen = linked(doc, near) == 0.0

    @pl.when(seen)
    def _():
        for j in range(features // HD):
            head = pl.ds(j * HD, HD)
            k = kv_before[0, :, head]
            v = kv_before[1, :, head]
            for h in range(0, GROUP, 2):
                first = (j * GROUP + h) * HD
                at = pl.ds(first, CHUNK)
                top_here, total_here, dot_here = (stats[i : i + 1, at] for i in range(3))
                logits = dot_t(k, lanes(q, first, 2)) * LOG2_SCALE
                top = jnp.maximum(jnp.max(logits, axis=0, keepdims=True), top_here)
                e = jnp.exp2(logits - top)
                dp = dot_t(v, lanes(do, first, 2))
                shrink = jnp.exp2(top_here - top)
                ratio = 1.0 / (total_here * shrink + jnp.sum(e, axis=0, keepdims=True))
                delta = (dot_here * shrink + jnp.sum(e * dp, axis=0, keepdims=True)) * ratio
                prob = e * ratio
                p[:, at] = prob.astype(BF16)
                ds[:, at] = (prob * (dp - delta)).astype(BF16)
                after[0:1, at] = shrink * ratio
                after[1:2, at] = delta
        for j in range(features // HD):
            head = pl.ds(j * HD, HD)
            cols = pl.ds(j * GROUP * HD, GROUP * HD)
            dk = dot(ds[:, cols], lanes(q, j * GROUP * HD, GROUP)) * SCALE
            dv = dot(p[:, cols], lanes(do, j * GROUP * HD, GROUP))
            before[0, :, head] = dk.astype(BF16)
            before[1, :, head] = dv.astype(BF16)

    @pl.when(jnp.logical_not(seen))
    def _():
        before[...] = jnp.zeros_like(before)
        p[...] = jnp.zeros_like(p)
        ds[...] = jnp.zeros_like(ds)
        ratio = 1.0 / stats[1:2, :]
        after[0:1, :] = ratio
        after[1:2, :] = stats[2:3, :] * ratio


def cross(doc, kv_before, queries, out_grad, stats, behind):
    _, piece_len, features = kv_before.shape
    width = queries.shape[3]
    return pl.pallas_call(
        cross_kernel,
        out_shape=(
            pltpu.VMEM((2, piece_len, features), BF16),
            pltpu.VMEM((piece_len, width), BF16),
            pltpu.VMEM((piece_len, width), BF16),
            pltpu.VMEM((8, width), F32),
        ),
        in_specs=[in_smem] + [in_vmem] * 5,
        out_specs=(in_vmem,) * 4,
        compiler_params=pltpu.CompilerParams(vmem_limit_bytes=VMEM_LIMIT),
        name="cross",
    )(doc, kv_before, queries, out_grad, stats, behind)


def turn(wide, ref, first):
    for i in range(wide.shape[1] // HD):
        ref[:, pl.ds(first + i * HD, HD)] = wide[:, i * HD : (i + 1) * HD].T


def rest_kernel(*refs):
    near_kv, queries, out_grad, weights, dprobs, after, far_kv, mate_kv, p_far, ds_far = refs[:10]
    next_kv, p_next, ds_next = refs[10:13]
    out, q_grad, own, o, dq, p, ds, sems = refs[-8:]
    near, far = near_slot(), far_slot()
    q, do = queries.at[near, 0], out_grad.at[near, 0]
    kv_heads = near_kv.shape[2] // HD
    span = GROUP * HD
    backs = []

    def give_back(side, slot, j):
        cols = pl.ds(j * span, span)
        for n, (a, b) in enumerate(((o, out), (dq, q_grad))):
            sem = sems.at[(side * kv_heads + j) * 2 + n]
            back = pltpu.make_async_copy(a.at[side, :, cols], b.at[slot, 0, :, cols], sem)
            back.start()
            backs.append(back)

    for j in range(kv_heads):
        head = pl.ds(j * HD, HD)
        k_t = jnp.concatenate([mate_kv[0, :, head], far_kv[0, :, head]], axis=0).T
        v_t = jnp.concatenate([mate_kv[1, :, head], far_kv[1, :, head]], axis=0).T
        for h in range(0, GROUP, 2):
            first = (j * GROUP + h) * HD
            at = pl.ds(first, CHUNK)
            turn(dot(v_t, p_far[:, at]).astype(BF16), o.at[1], first)
            turn((dot(k_t, ds_far[:, at]) * SCALE).astype(BF16), dq.at[1], first)
        give_back(1, far, j)
    for j in range(kv_heads):
        head = pl.ds(j * HD, HD)
        k_t = jnp.concatenate([next_kv[0, :, head], near_kv[0, :, head]], axis=0).T
        v_t = jnp.concatenate([next_kv[1, :, head], near_kv[1, :, head]], axis=0).T
        for h in range(0, GROUP, 2):
            first = (j * GROUP + h) * HD
            at = pl.ds(first, CHUNK)
            prob = weights[:, at] * after[0:1, at]
            prob_low = prob.astype(BF16)
            ds_low = (prob * (dprobs[:, at] - after[1:2, at])).astype(BF16)
            p[:, pl.ds(h * HD, CHUNK)] = prob_low
            ds[:, pl.ds(h * HD, CHUNK)] = ds_low
            prob_low = jnp.concatenate([p_next[:, at], prob_low], axis=0)
            ds_low = jnp.concatenate([ds_next[:, at], ds_low], axis=0)
            turn(dot(v_t, prob_low).astype(BF16), o.at[0], first)
            turn((dot(k_t, ds_low) * SCALE).astype(BF16), dq.at[0], first)
        give_back(0, near, j)
        own[0, :, head] = dot(ds[...], lanes(q, j * span, GROUP)) * SCALE
        own[1, :, head] = dot(p[...], lanes(do, j * span, GROUP))
    for back in backs:
        back.wait()


def rest(*operands, shape):
    _, piece_len, features = operands[0].shape
    width = shape[3]
    kv_heads = features // HD
    wide = pltpu.HBM(shape, BF16)
    return pl.pallas_call(
        rest_kernel,
        out_shape=(wide, wide, pltpu.VMEM((2, piece_len, features), F32)),
        in_specs=[in_vmem] * len(operands),
        out_specs=(in_hbm, in_hbm, in_vmem),
        scratch_shapes=[pltpu.VMEM((2, piece_len, width), BF16)] * 2
        + [pltpu.VMEM((piece_len, GROUP * HD), BF16)] * 2
        + [pltpu.SemaphoreType.DMA((4 * kv_heads,))],
        compiler_params=pltpu.CompilerParams(vmem_limit_bytes=VMEM_LIMIT),
        name="rest",
    )(*operands)


def far_side_kernel(far_kv, mate_kv, p_far, ds_far, o, dq):
    for j in range(far_kv.shape[2] // HD):
        head = pl.ds(j * HD, HD)
        k_t = jnp.concatenate([mate_kv[0, :, head], far_kv[0, :, head]], axis=0).T
        v_t = jnp.concatenate([mate_kv[1, :, head], far_kv[1, :, head]], axis=0).T
        for h in range(0, GROUP, 2):
            first = (j * GROUP + h) * HD
            at = pl.ds(first, CHUNK)
            turn(dot(v_t, p_far[:, at]).astype(BF16), o, first)
            turn((dot(k_t, ds_far[:, at]) * SCALE).astype(BF16), dq, first)


def far_side(far_kv, mate_kv, p_far, ds_far):
    shape = pltpu.VMEM((far_kv.shape[1], p_far.shape[1]), BF16)
    return pl.pallas_call(
        far_side_kernel,
        out_shape=(shape, shape),
        in_specs=[in_vmem] * 4,
        out_specs=(in_vmem,) * 2,
        compiler_params=pltpu.CompilerParams(vmem_limit_bytes=VMEM_LIMIT),
        name="far_side",
    )(far_kv, mate_kv, p_far, ds_far)


def last_kernel(
    near_kv, queries, out_grad, weights, dprobs, stats, o_far, dq_far, far_own, near_back,
    out, q_grad, k_grad, v_grad, o, dq, p, ds, k_low, v_low, sems,
):
    near, far = near_slot(), far_slot()
    q, do = queries.at[near, 0], out_grad.at[near, 0]
    span = GROUP * HD
    moves = [(o_far, out.at[far, 0]), (dq_far, q_grad.at[far, 0])]
    backs = fetch_pairs(moves, sems)
    for j in range(near_kv.shape[2] // HD):
        head = pl.ds(j * HD, HD)
        k_t, v_t = near_kv[0, :, head].T, near_kv[1, :, head].T
        for h in range(0, GROUP, 2):
            first = (j * GROUP + h) * HD
            at = pl.ds(first, CHUNK)
            ratio = 1.0 / stats[1:2, at]
            prob = weights[:, at] * ratio
            prob_low = prob.astype(BF16)
            ds_low = (prob * (dprobs[:, at] - stats[2:3, at] * ratio)).astype(BF16)
            p[:, at] = prob_low
            ds[:, at] = ds_low
            turn(dot(v_t, prob_low).astype(BF16), o, first)
            turn((dot(k_t, ds_low) * SCALE).astype(BF16), dq, first)
        cols = pl.ds(j * span, span)
        for a, b in ((o, out), (dq, q_grad)):
            back = pltpu.make_async_copy(a.at[:, cols], b.at[near, 0, :, cols], sems.at[len(backs)])
            back.start()
            backs.append(back)
    for j in range(near_kv.shape[2] // HD):
        head = pl.ds(j * HD, HD)
        cols = pl.ds(j * span, span)
        dk = dot(ds[:, cols], lanes(q, j * span, GROUP)) * SCALE
        dv = dot(p[:, cols], lanes(do, j * span, GROUP))
        k_low[near, 0, :, head] = (dk + near_back[0, :, head].astype(F32)).astype(BF16)
        v_low[near, 0, :, head] = (dv + near_back[1, :, head].astype(F32)).astype(BF16)
    k_low[far, 0] = far_own[0].astype(BF16)
    v_low[far, 0] = far_own[1].astype(BF16)
    for a, b in ((k_low, k_grad), (v_low, v_grad)):
        back = pltpu.make_async_copy(a, b, sems.at[len(backs)])
        back.start()
        backs.append(back)
    for back in backs:
        back.wait()


def last(*operands):
    _, piece_len, features = operands[0].shape
    shape = operands[1].shape
    small = (2, 1, piece_len, features)
    kv_heads = features // HD
    return pl.pallas_call(
        last_kernel,
        out_shape=(pltpu.HBM(shape, BF16),) * 2 + (pltpu.HBM(small, BF16),) * 2,
        in_specs=[in_vmem] * len(operands),
        out_specs=(in_hbm,) * 4,
        scratch_shapes=[pltpu.VMEM((piece_len, shape[3]), BF16)] * 4
        + [pltpu.VMEM(small, BF16)] * 2
        + [pltpu.SemaphoreType.DMA((4 + 2 * kv_heads,))],
        compiler_params=pltpu.CompilerParams(vmem_limit_bytes=VMEM_LIMIT),
        name="last",
    )(*operands)


def total_kernel(near_own, far_own, near_back, far_back, k_grad, v_grad, k_low, v_low, sems):
    near, far = near_slot(), far_slot()
    for n, low in enumerate((k_low, v_low)):
        low[near, 0] = (near_own[n] + near_back[n].astype(F32)).astype(BF16)
        low[far, 0] = (far_own[n] + far_back[n].astype(F32)).astype(BF16)
    for copy in fetch_pairs([(k_low, k_grad), (v_low, v_grad)], sems):
        copy.wait()


def total(*operands):
    _, piece_len, features = operands[0].shape
    shape = (2, 1, piece_len, features)
    return pl.pallas_call(
        total_kernel,
        out_shape=(pltpu.HBM(shape, BF16),) * 2,
        in_specs=[in_vmem] * len(operands),
        out_specs=(in_hbm,) * 2,
        scratch_shapes=[pltpu.VMEM(shape, BF16)] * 2 + [pltpu.SemaphoreType.DMA((2,))],
        compiler_params=pltpu.CompilerParams(vmem_limit_bytes=VMEM_LIMIT),
        name="total",
    )(*operands)


def far_links(pairs):
    low = [(i, i + 1, i) for i in range(3, pairs - 1, 2)]
    high = [(i + 1, i, 2 * pairs - 2 - i) for i in range(1, pairs - 3, 2)]
    return low + high


def hops(flow):
    (y, x, core), (to_y, to_x, to_core) = ((i // 4, i // 2 % 2, i % 2) for i in flow)
    steps = []
    if x != to_x:
        steps.append(("x", to_x, y))
    if y != to_y:
        steps.append(("y", to_y, to_x))
    return steps, core != to_core


def burden(flow, taken, late):
    steps, other_core = hops(flow)
    weight = 0.1
    if steps:
        weight = len(steps) + 0.3 * other_core + (1.5 if flow[1] == 0 else 0.5 * (flow[1] % 2))
        weight += 3.0 * sum(step in taken for step in steps)
        weight += 0.7 * (flow[1] in late)
    return weight


SPARE = {
    ((5, 6), (2, 1)): [(3, 2), (4, 5), (6, 7), (1, 0), (0, 3), (7, 4)],
    ((6, 5), (1, 2)): [(2, 3), (5, 4), (7, 6), (0, 1), (3, 0), (4, 7)],
}


def complete(route, pairs):
    if pairs == 8 and tuple(route) in SPARE:
        return route + SPARE[tuple(route)]
    sources = [i for i in range(pairs) if i not in {a for a, _ in route}]
    targets = [i for i in range(pairs) if i not in {b for _, b in route}]
    if pairs == 8:
        taken = {step for flow in route for step in hops(flow)[0]}
        late = {i for flow in route for i in flow}
        found = [(math.inf, [])]

        def search(rest_of, free, cost, chosen):
            if cost >= found[0][0]:
                return
            if not rest_of:
                found[0] = (cost, chosen)
                return
            for b in free:
                flow = (rest_of[0], b)
                if flow[0] != b:
                    left = [t for t in free if t != b]
                    more = burden(flow, taken, late)
                    search(rest_of[1:], left, cost + more, chosen + [flow])

        search(sources, targets, 0.0, [])
        if found[0][0] < math.inf:
            return route + found[0][1]
    for turn_by in range(len(targets)):
        turned = targets[turn_by:] + targets[:turn_by]
        if all(a != b for a, b in zip(sources, turned)):
            return route + list(zip(sources, turned))
    return route


def attend_pairs(links, queries, out_grad, doc, far_kv, near_kv):
    pairs = lax.axis_size("ctx")
    mates = [(i, i ^ 1) for i in range(pairs) if i ^ 1 < pairs]
    flows = [(a, b) for a, b, _ in links]
    far_kv, near_kv = keep(far_kv, near_kv)
    mate_kv = lax.ppermute(near_kv, "ctx", mates)
    if links:
        next_kv = lax.ppermute(far_kv, "ctx", complete(flows, pairs))
    weights, dprobs, stats = diagonal(doc, near_kv, queries, out_grad)
    mate_grads, far_own, p_far, ds_far = whole(stats, far_kv, mate_kv, queries, out_grad)
    mate_back = lax.ppermute(mate_grads, "ctx", mates)
    if not links:
        o_far, dq_far = far_side(far_kv, mate_kv, p_far, ds_far)
        return last(
            near_kv, queries, out_grad, weights, dprobs, stats, o_far, dq_far, far_own, mate_back
        )
    next_grads, p_next, ds_next, after = cross(
        doc, next_kv, queries, out_grad, stats, mate_grads
    )
    far_back = lax.ppermute(next_grads, "ctx", complete([(b, a) for a, b in flows], pairs))
    out, q_grad, near_own = rest(
        near_kv, queries, out_grad, weights, dprobs, after, far_kv, mate_kv, p_far, ds_far,
        next_kv, p_next, ds_next, shape=queries.shape,
    )
    k_grad, v_grad = total(near_own, far_own, mate_back, far_back)
    return (out, q_grad, k_grad, v_grad)


def local_pairs(queries, keys, values, out_grad, block_doc):
    links = far_links(lax.axis_size("ctx"))
    low = [link for link in links if link[0] < link[1]]
    high = [link for link in links if link[0] > link[1]]
    outer = [link for link in links if min(link[:2]) % 4 == 3]
    inner = [link for link in links if min(link[:2]) % 4 == 1]

    def needed(doc):
        def linked_among(*groups):
            some = [link for link in links if all(link in group for group in groups)]
            same = [doc[first] == doc[first + 1] for _, _, first in some]
            return functools.reduce(jnp.logical_or, same)

        any_outer = linked_among(outer)
        any_low, any_high = linked_among(low), linked_among(high)
        side = jnp.where(any_low, jnp.where(any_high, 4, 2), 3)
        near_only = jnp.where(linked_among(inner), 1, 0)
        return jnp.where(any_outer, side, near_only)

    far_kv, near_kv, case, doc = pick(keys, values, block_doc, needed)
    branches = [functools.partial(attend_pairs, some) for some in ([], inner, low, high, links)]
    return lax.switch(case[0], branches, queries, out_grad, doc, far_kv, near_kv)


def local(queries, keys, values, out_grad, block_doc):
    window = min(7, lax.axis_size("ctx") // 4 - 1) + 1
    piece_len = queries.shape[2]
    even = lax.axis_size("ctx") % 2 == 0
    if window == 2 and piece_len == BLOCK and even:
        return local_pairs(queries, keys, values, out_grad, block_doc)
    return local_wide(queries, keys, values, out_grad, block_doc)


def solution(mesh):
    in_specs = (
        P(None, "ctx", None, "tp"),
        P(None, "ctx", None, "tp"),
        P(None, "ctx", None, "tp"),
        P(None, "ctx", None, "tp"),
        P(),
    )
    out_specs = (
        P(None, "ctx", None, "tp"),
        P(None, "ctx", None, "tp"),
        P(None, "ctx", None, "tp"),
        P(None, "ctx", None, "tp"),
    )
    return jax.shard_map(local, mesh=mesh, in_specs=in_specs, out_specs=out_specs, check_vma=False)
```

```python
import functools
import math

import jax
import jax.numpy as jnp
from jax import lax
from jax.experimental import pallas as pl
from jax.experimental.pallas import tpu as pltpu
from jax.sharding import PartitionSpec as P

HQ = 64
HK = 8
HD = 128
BLOCK = 128


masked_score = -1e30


def shifted(block, axis, distance):
    devices = range(lax.axis_size(axis))
    route = [(i - distance, i) for i in devices if i - distance in devices]
    return lax.ppermute(block, axis, route)


def move_keys(payload, distance):
    return shifted(payload, "ctx", distance)


def move_grads(payload, distance):
    return shifted(payload.astype(jnp.bfloat16), "ctx", distance).astype(payload.dtype)


def piece_docs(block_doc, piece_index, piece_len):
    per_piece = piece_len // BLOCK
    start = jnp.maximum(piece_index, 0) * per_piece
    doc_blocks = lax.dynamic_slice_in_dim(block_doc, start, per_piece, 0)
    doc_tokens = jnp.repeat(doc_blocks, BLOCK)
    return jnp.where(piece_index >= 0, doc_tokens, -1)


def attend(query_piece, grad_piece, key_buffer, piece_index, block_doc):
    window, _, piece_len, features = key_buffer.shape
    kv_heads = features // HD
    scaling = 1.0 / math.sqrt(HD)
    key_slots = key_buffer[:, 0].reshape(window, piece_len, kv_heads, HD)
    value_slots = key_buffer[:, 1].reshape(window, piece_len, kv_heads, HD)
    keys_flat = key_slots.reshape(window * piece_len, kv_heads, HD)
    values_flat = value_slots.reshape(window * piece_len, kv_heads, HD)
    positions = jnp.arange(piece_len, dtype=jnp.int32)
    query_docs = piece_docs(block_doc, piece_index, piece_len)
    query_pos = piece_index * piece_len + positions
    visible_rows = []
    for slot_index in range(window):
        key_index = piece_index - (window - 1) + slot_index
        key_docs = piece_docs(block_doc, key_index, piece_len)
        key_pos = key_index * piece_len + positions
        visible_rows.append(
            (key_docs[None, :] == query_docs[:, None]) & (key_pos[None, :] <= query_pos[:, None])
        )
    visible = jnp.concatenate(visible_rows, axis=1)

    def key_side(form, left, flat):
        return jnp.einsum(form, left, flat, preferred_element_type=jnp.float32)

    def key_sum(form, weights, flat):
        return jnp.einsum(form, weights, flat, preferred_element_type=jnp.float32)

    def per_key(form, weights, right):
        return jnp.einsum(form, weights, right, preferred_element_type=jnp.float32).reshape(
            window, piece_len, kv_heads, HD
        )

    raw_scores = key_side("qhgd,khd->hgqk", query_piece, keys_flat)
    scores = jnp.where(visible[None, None], raw_scores * scaling, masked_score)
    row_max = jnp.max(scores, axis=-1, keepdims=True)
    log_total = row_max + jnp.log(jnp.sum(jnp.exp(scores - row_max), axis=-1, keepdims=True))
    probs = jnp.exp(scores - log_total)
    probs_low = probs.astype(jnp.bfloat16)
    attended = key_sum("hgqk,khd->qhgd", probs_low, values_flat)
    out_low = attended.astype(jnp.bfloat16)
    out_back = lax.optimization_barrier(out_low).astype(jnp.float32)
    delta = jnp.einsum("qhgd,qhgd->hgq", grad_piece.astype(jnp.float32), out_back)
    dprobs = key_side("qhgd,khd->hgqk", grad_piece, values_flat)
    dscores = (probs * (dprobs - delta[..., None])).astype(jnp.bfloat16)
    query_part = (key_sum("hgqk,khd->qhgd", dscores, keys_flat) * scaling).astype(jnp.bfloat16)
    key_part = per_key("hgqk,qhgd->khd", dscores, query_piece) * scaling
    value_part = per_key("hgqk,qhgd->khd", probs_low, grad_piece)
    grads = jnp.stack(
        [
            key_part.reshape(window, piece_len, features),
            value_part.reshape(window, piece_len, features),
        ],
        axis=1,
    )
    return (out_low.reshape(piece_len, -1), query_part.reshape(piece_len, -1), grads)


def local_wide(queries, keys, values, out_grad, block_doc):
    ctx_size = lax.axis_size("ctx")
    my_index = lax.axis_index("ctx")
    reach_back = min(7, ctx_size // 4 - 1)
    window = reach_back + 1
    levels = window.bit_length() - 1
    piece_len = queries.shape[2]
    kv_heads = keys.shape[3] // HD
    group = HQ // HK
    query_all = queries[:, 0].reshape(2, piece_len, kv_heads, group, HD)
    grad_all = out_grad[:, 0].reshape(2, piece_len, kv_heads, group, HD)
    paired = jnp.stack([keys[:, 0], values[:, 0]], axis=1)
    low_buffer = paired[0][None]
    high_buffer = paired[1][None]
    for level_bit in range(levels):
        distance = 1 << level_bit
        low_buffer = jnp.concatenate([move_keys(low_buffer, distance), low_buffer], axis=0)
        high_buffer = jnp.concatenate([move_keys(high_buffer, -distance), high_buffer], axis=0)
    high_index = 2 * ctx_size - 1 - my_index
    low_out, low_qgrad, low_grads = attend(
        query_all[0], grad_all[0], low_buffer, my_index, block_doc
    )
    high_out, high_qgrad, high_grads = attend(
        query_all[1], grad_all[1], high_buffer, high_index, block_doc
    )
    low_back = low_grads
    high_back = high_grads
    for level_bit in reversed(range(levels)):
        distance = 1 << level_bit
        low_back = low_back[distance:] + move_grads(low_back[:distance], -distance)
        high_back = high_back[distance:] + move_grads(high_back[:distance], distance)
    low_total = low_back[0]
    high_total = high_back[0]
    attn_pair = jnp.stack([low_out, high_out])[:, None]
    qgrad_pair = jnp.stack([low_qgrad, high_qgrad])[:, None]
    key_pair = jnp.stack([low_total[0], high_total[0]]).astype(jnp.bfloat16)[:, None]
    value_pair = jnp.stack([low_total[1], high_total[1]]).astype(jnp.bfloat16)[:, None]
    return (attn_pair, qgrad_pair, key_pair, value_pair)


GROUP = HQ // HK
CHUNK = 2 * HD
LOG2_SCALE = math.log2(math.e) / math.sqrt(HD)
SCALE = 1.0 / math.sqrt(HD)
VMEM_LIMIT = 24 * 1024 * 1024

F32 = jnp.float32
BF16 = jnp.bfloat16

in_vmem = pl.BlockSpec(memory_space=pltpu.VMEM)
in_hbm = pl.BlockSpec(memory_space=pltpu.HBM)
in_smem = pl.BlockSpec(memory_space=pltpu.SMEM)


def dot(left, right):
    return jnp.dot(left, right, preferred_element_type=F32)


def dot_t(left, right):
    return lax.dot_general(left, right, (((1,), (1,)), ((), ())), preferred_element_type=F32)


def near_slot():
    return lax.rem(lax.axis_index("ctx"), 2)


def far_slot():
    return 1 - near_slot()


def linked(doc_ref, slot):
    pairs = lax.axis_size("ctx")
    me = lax.axis_index("ctx")
    piece = jnp.where(slot == 0, me, 2 * pairs - 1 - me)
    same = doc_ref[piece] == doc_ref[jnp.maximum(piece - 1, 0)]
    return jnp.where(jnp.logical_and(piece > 0, same), 0.0, masked_score).astype(F32)


def lanes(ref, first, count):
    parts = [ref[:, pl.ds(first + i * HD, HD)] for i in range(count)]
    return jnp.concatenate(parts, axis=0)


def causal(rows, columns):
    key = lax.broadcasted_iota(jnp.int32, (rows, columns), 0)
    query = lax.broadcasted_iota(jnp.int32, (rows, columns), 1)
    return key <= lax.rem(query, rows)


def fetch_pairs(pairs_of_refs, sems):
    copies = [pltpu.make_async_copy(a, b, sems.at[i]) for i, (a, b) in enumerate(pairs_of_refs)]
    for copy in copies:
        copy.start()
    return copies


def pick_kernel(needed, keys, values, block_doc, far_kv, near_kv, case, doc, sems):
    far, near = far_slot(), near_slot()
    copies = fetch_pairs(
        [
            (block_doc, doc),
            (keys.at[far, 0], far_kv.at[0]),
            (values.at[far, 0], far_kv.at[1]),
            (keys.at[near, 0], near_kv.at[0]),
            (values.at[near, 0], near_kv.at[1]),
        ],
        sems,
    )
    copies[0].wait()
    case[0] = needed(doc)
    for copy in copies[1:]:
        copy.wait()


def pick(keys, values, block_doc, needed):
    _, _, piece_len, features = keys.shape
    shape = pltpu.VMEM((2, piece_len, features), BF16)
    return pl.pallas_call(
        functools.partial(pick_kernel, needed),
        out_shape=(
            shape,
            shape,
            pltpu.SMEM((1,), jnp.int32),
            pltpu.SMEM(block_doc.shape, jnp.int32),
        ),
        in_specs=[in_hbm, in_hbm, in_hbm],
        out_specs=(in_vmem, in_vmem, in_smem, in_smem),
        scratch_shapes=[pltpu.SemaphoreType.DMA((5,))],
        name="pick",
    )(keys, values, block_doc)


def keep_kernel(*refs):
    pass


def keep(far_kv, near_kv):
    shape = pltpu.VMEM(far_kv.shape, BF16)
    return pl.pallas_call(
        keep_kernel,
        out_shape=(shape, shape),
        in_specs=[in_vmem, in_vmem],
        out_specs=(in_vmem, in_vmem),
        input_output_aliases={0: 0, 1: 1},
        cost_estimate=pl.CostEstimate(flops=10**10, bytes_accessed=10**6, transcendentals=0),
        compiler_params=pltpu.CompilerParams(vmem_limit_bytes=VMEM_LIMIT),
        name="keep",
    )(far_kv, near_kv)


def diagonal_kernel(doc, kv, queries, out_grad, weights, dprobs, stats):
    near = near_slot()
    q, do = queries.at[near, 0], out_grad.at[near, 0]
    kv_heads = kv.shape[2] // HD
    bias = linked(doc, near)
    bias_far = linked(doc, 1 - near)
    mask = causal(kv.shape[1], CHUNK)
    for j in range(kv_heads):
        k = kv[0, :, pl.ds(j * HD, HD)]
        v = kv[1, :, pl.ds(j * HD, HD)]
        for h in range(0, GROUP, 2):
            first = (j * GROUP + h) * HD
            at = pl.ds(first, CHUNK)
            logits = jnp.where(mask, dot_t(k, lanes(q, first, 2)) * LOG2_SCALE, masked_score)
            top = jnp.max(logits, axis=0, keepdims=True)
            e = jnp.exp2(logits - top)
            dp = dot_t(v, lanes(do, first, 2))
            weights[:, at] = e
            dprobs[:, at] = dp
            stats[0:1, at] = top
            stats[1:2, at] = jnp.sum(e, axis=0, keepdims=True)
            stats[2:3, at] = jnp.sum(e * dp, axis=0, keepdims=True)
            stats[3:4, at] = jnp.full((1, CHUNK), bias, F32)
            stats[4:5, at] = jnp.full((1, CHUNK), bias_far, F32)


def diagonal(block_doc, kv, queries, out_grad):
    _, _, piece_len, width = queries.shape
    return pl.pallas_call(
        diagonal_kernel,
        out_shape=(
            pltpu.VMEM((piece_len, width), F32),
            pltpu.VMEM((piece_len, width), F32),
            pltpu.VMEM((8, width), F32),
        ),
        in_specs=[in_smem, in_vmem, in_vmem, in_vmem],
        out_specs=(in_vmem,) * 3,
        compiler_params=pltpu.CompilerParams(vmem_limit_bytes=VMEM_LIMIT),
        name="diagonal",
    )(block_doc, kv, queries, out_grad)


def whole_kernel(stats, kv, kv_before, queries, out_grad, before, own, p, ds):
    far = far_slot()
    q, do = queries.at[far, 0], out_grad.at[far, 0]
    kv_heads = kv.shape[2] // HD
    piece_len = kv.shape[1]
    bias = stats[4:5, :CHUNK]
    mask = causal(piece_len, CHUNK)
    for j in range(kv_heads):
        head = pl.ds(j * HD, HD)
        k = jnp.concatenate([kv_before[0, :, head], kv[0, :, head]], axis=0)
        v = jnp.concatenate([kv_before[1, :, head], kv[1, :, head]], axis=0)
        for h in range(0, GROUP, 2):
            first = (j * GROUP + h) * HD
            at = pl.ds(first, CHUNK)
            logits = dot_t(k, lanes(q, first, 2)) * LOG2_SCALE
            cross = logits[:piece_len]
            here = jnp.where(mask, logits[piece_len:], masked_score)
            top = jnp.maximum(
                jnp.max(cross, axis=0, keepdims=True) + bias, jnp.max(here, axis=0, keepdims=True)
            )
            e = jnp.concatenate([jnp.exp2(cross - (top - bias)), jnp.exp2(here - top)], axis=0)
            dp = dot_t(v, lanes(do, first, 2))
            ratio = 1.0 / jnp.sum(e, axis=0, keepdims=True)
            delta = jnp.sum(e * dp, axis=0, keepdims=True) * ratio
            prob = e * ratio
            p[:, at] = prob.astype(BF16)
            ds[:, at] = (prob * (dp - delta)).astype(BF16)
    for j in range(kv_heads):
        head = pl.ds(j * HD, HD)
        cols = pl.ds(j * GROUP * HD, GROUP * HD)
        dk = dot(ds[:, cols], lanes(q, j * GROUP * HD, GROUP)) * SCALE
        dv = dot(p[:, cols], lanes(do, j * GROUP * HD, GROUP))
        before[0, :, head] = dk[:piece_len].astype(BF16)
        before[1, :, head] = dv[:piece_len].astype(BF16)
        own[0, :, head] = dk[piece_len:]
        own[1, :, head] = dv[piece_len:]


def whole(stats, kv, kv_before, queries, out_grad):
    _, piece_len, features = kv.shape
    width = queries.shape[3]
    return pl.pallas_call(
        whole_kernel,
        out_shape=(
            pltpu.VMEM((2, piece_len, features), BF16),
            pltpu.VMEM((2, piece_len, features), F32),
            pltpu.VMEM((2 * piece_len, width), BF16),
            pltpu.VMEM((2 * piece_len, width), BF16),
        ),
        in_specs=[in_vmem] * 5,
        out_specs=(in_vmem,) * 4,
        compiler_params=pltpu.CompilerParams(vmem_limit_bytes=VMEM_LIMIT),
        name="whole",
    )(stats, kv, kv_before, queries, out_grad)


def cross_kernel(doc, kv_before, queries, out_grad, stats, behind, before, p, ds, after):
    near = near_slot()
    q, do = queries.at[near, 0], out_grad.at[near, 0]
    piece_len, features = kv_before.shape[1:]
    seen = linked(doc, near) == 0.0

    @pl.when(seen)
    def _():
        for j in range(features // HD):
            head = pl.ds(j * HD, HD)
            k = kv_before[0, :, head]
            v = kv_before[1, :, head]
            for h in range(0, GROUP, 2):
                first = (j * GROUP + h) * HD
                at = pl.ds(first, CHUNK)
                top_here, total_here, dot_here = (stats[i : i + 1, at] for i in range(3))
                logits = dot_t(k, lanes(q, first, 2)) * LOG2_SCALE
                top = jnp.maximum(jnp.max(logits, axis=0, keepdims=True), top_here)
                e = jnp.exp2(logits - top)
                dp = dot_t(v, lanes(do, first, 2))
                shrink = jnp.exp2(top_here - top)
                ratio = 1.0 / (total_here * shrink + jnp.sum(e, axis=0, keepdims=True))
                delta = (dot_here * shrink + jnp.sum(e * dp, axis=0, keepdims=True)) * ratio
                prob = e * ratio
                p[:, at] = prob.astype(BF16)
                ds[:, at] = (prob * (dp - delta)).astype(BF16)
                after[0:1, at] = shrink * ratio
                after[1:2, at] = delta
        for j in range(features // HD):
            head = pl.ds(j * HD, HD)
            cols = pl.ds(j * GROUP * HD, GROUP * HD)
            dk = dot(ds[:, cols], lanes(q, j * GROUP * HD, GROUP)) * SCALE
            dv = dot(p[:, cols], lanes(do, j * GROUP * HD, GROUP))
            before[0, :, head] = dk.astype(BF16)
            before[1, :, head] = dv.astype(BF16)

    @pl.when(jnp.logical_not(seen))
    def _():
        before[...] = jnp.zeros_like(before)
        p[...] = jnp.zeros_like(p)
        ds[...] = jnp.zeros_like(ds)
        ratio = 1.0 / stats[1:2, :]
        after[0:1, :] = ratio
        after[1:2, :] = stats[2:3, :] * ratio


def cross(doc, kv_before, queries, out_grad, stats, behind):
    _, piece_len, features = kv_before.shape
    width = queries.shape[3]
    return pl.pallas_call(
        cross_kernel,
        out_shape=(
            pltpu.VMEM((2, piece_len, features), BF16),
            pltpu.VMEM((piece_len, width), BF16),
            pltpu.VMEM((piece_len, width), BF16),
            pltpu.VMEM((8, width), F32),
        ),
        in_specs=[in_smem] + [in_vmem] * 5,
        out_specs=(in_vmem,) * 4,
        compiler_params=pltpu.CompilerParams(vmem_limit_bytes=VMEM_LIMIT),
        name="cross",
    )(doc, kv_before, queries, out_grad, stats, behind)


def turn(wide, ref, first):
    for i in range(wide.shape[1] // HD):
        ref[:, pl.ds(first + i * HD, HD)] = wide[:, i * HD : (i + 1) * HD].T


def rest_kernel(*refs):
    near_kv, queries, out_grad, weights, dprobs, after, far_kv, mate_kv, p_far, ds_far = refs[:10]
    next_kv, p_next, ds_next = refs[10:13]
    out, q_grad, own, o, dq, p, ds, sems = refs[-8:]
    near, far = near_slot(), far_slot()
    q, do = queries.at[near, 0], out_grad.at[near, 0]
    kv_heads = near_kv.shape[2] // HD
    span = GROUP * HD
    backs = []

    def give_back(side, slot, j):
        cols = pl.ds(j * span, span)
        for n, (a, b) in enumerate(((o, out), (dq, q_grad))):
            sem = sems.at[(side * kv_heads + j) * 2 + n]
            back = pltpu.make_async_copy(a.at[side, :, cols], b.at[slot, 0, :, cols], sem)
            back.start()
            backs.append(back)

    for j in range(kv_heads):
        head = pl.ds(j * HD, HD)
        k_t = jnp.concatenate([mate_kv[0, :, head], far_kv[0, :, head]], axis=0).T
        v_t = jnp.concatenate([mate_kv[1, :, head], far_kv[1, :, head]], axis=0).T
        for h in range(0, GROUP, 2):
            first = (j * GROUP + h) * HD
            at = pl.ds(first, CHUNK)
            turn(dot(v_t, p_far[:, at]).astype(BF16), o.at[1], first)
            turn((dot(k_t, ds_far[:, at]) * SCALE).astype(BF16), dq.at[1], first)
        give_back(1, far, j)
    for j in range(kv_heads):
        head = pl.ds(j * HD, HD)
        k_t = jnp.concatenate([next_kv[0, :, head], near_kv[0, :, head]], axis=0).T
        v_t = jnp.concatenate([next_kv[1, :, head], near_kv[1, :, head]], axis=0).T
        for h in range(0, GROUP, 2):
            first = (j * GROUP + h) * HD
            at = pl.ds(first, CHUNK)
            prob = weights[:, at] * after[0:1, at]
            prob_low = prob.astype(BF16)
            ds_low = (prob * (dprobs[:, at] - after[1:2, at])).astype(BF16)
            p[:, pl.ds(h * HD, CHUNK)] = prob_low
            ds[:, pl.ds(h * HD, CHUNK)] = ds_low
            prob_low = jnp.concatenate([p_next[:, at], prob_low], axis=0)
            ds_low = jnp.concatenate([ds_next[:, at], ds_low], axis=0)
            turn(dot(v_t, prob_low).astype(BF16), o.at[0], first)
            turn((dot(k_t, ds_low) * SCALE).astype(BF16), dq.at[0], first)
        give_back(0, near, j)
        own[0, :, head] = dot(ds[...], lanes(q, j * span, GROUP)) * SCALE
        own[1, :, head] = dot(p[...], lanes(do, j * span, GROUP))
    for back in backs:
        back.wait()


def rest(*operands, shape):
    _, piece_len, features = operands[0].shape
    width = shape[3]
    kv_heads = features // HD
    wide = pltpu.HBM(shape, BF16)
    return pl.pallas_call(
        rest_kernel,
        out_shape=(wide, wide, pltpu.VMEM((2, piece_len, features), F32)),
        in_specs=[in_vmem] * len(operands),
        out_specs=(in_hbm, in_hbm, in_vmem),
        scratch_shapes=[pltpu.VMEM((2, piece_len, width), BF16)] * 2
        + [pltpu.VMEM((piece_len, GROUP * HD), BF16)] * 2
        + [pltpu.SemaphoreType.DMA((4 * kv_heads,))],
        compiler_params=pltpu.CompilerParams(vmem_limit_bytes=VMEM_LIMIT),
        name="rest",
    )(*operands)


def far_side_kernel(far_kv, mate_kv, p_far, ds_far, o, dq):
    for j in range(far_kv.shape[2] // HD):
        head = pl.ds(j * HD, HD)
        k_t = jnp.concatenate([mate_kv[0, :, head], far_kv[0, :, head]], axis=0).T
        v_t = jnp.concatenate([mate_kv[1, :, head], far_kv[1, :, head]], axis=0).T
        for h in range(0, GROUP, 2):
            first = (j * GROUP + h) * HD
            at = pl.ds(first, CHUNK)
            turn(dot(v_t, p_far[:, at]).astype(BF16), o, first)
            turn((dot(k_t, ds_far[:, at]) * SCALE).astype(BF16), dq, first)


def far_side(far_kv, mate_kv, p_far, ds_far):
    shape = pltpu.VMEM((far_kv.shape[1], p_far.shape[1]), BF16)
    return pl.pallas_call(
        far_side_kernel,
        out_shape=(shape, shape),
        in_specs=[in_vmem] * 4,
        out_specs=(in_vmem,) * 2,
        compiler_params=pltpu.CompilerParams(vmem_limit_bytes=VMEM_LIMIT),
        name="far_side",
    )(far_kv, mate_kv, p_far, ds_far)


def last_kernel(
    near_kv, queries, out_grad, weights, dprobs, stats, o_far, dq_far, far_own, near_back,
    out, q_grad, k_grad, v_grad, o, dq, p, ds, k_low, v_low, sems,
):
    near, far = near_slot(), far_slot()
    q, do = queries.at[near, 0], out_grad.at[near, 0]
    span = GROUP * HD
    moves = [(o_far, out.at[far, 0]), (dq_far, q_grad.at[far, 0])]
    backs = fetch_pairs(moves, sems)
    for j in range(near_kv.shape[2] // HD):
        head = pl.ds(j * HD, HD)
        k_t, v_t = near_kv[0, :, head].T, near_kv[1, :, head].T
        for h in range(0, GROUP, 2):
            first = (j * GROUP + h) * HD
            at = pl.ds(first, CHUNK)
            ratio = 1.0 / stats[1:2, at]
            prob = weights[:, at] * ratio
            prob_low = prob.astype(BF16)
            ds_low = (prob * (dprobs[:, at] - stats[2:3, at] * ratio)).astype(BF16)
            p[:, at] = prob_low
            ds[:, at] = ds_low
            turn(dot(v_t, prob_low).astype(BF16), o, first)
            turn((dot(k_t, ds_low) * SCALE).astype(BF16), dq, first)
        cols = pl.ds(j * span, span)
        for a, b in ((o, out), (dq, q_grad)):
            back = pltpu.make_async_copy(a.at[:, cols], b.at[near, 0, :, cols], sems.at[len(backs)])
            back.start()
            backs.append(back)
    for j in range(near_kv.shape[2] // HD):
        head = pl.ds(j * HD, HD)
        cols = pl.ds(j * span, span)
        dk = dot(ds[:, cols], lanes(q, j * span, GROUP)) * SCALE
        dv = dot(p[:, cols], lanes(do, j * span, GROUP))
        k_low[near, 0, :, head] = (dk + near_back[0, :, head].astype(F32)).astype(BF16)
        v_low[near, 0, :, head] = (dv + near_back[1, :, head].astype(F32)).astype(BF16)
    k_low[far, 0] = far_own[0].astype(BF16)
    v_low[far, 0] = far_own[1].astype(BF16)
    for a, b in ((k_low, k_grad), (v_low, v_grad)):
        back = pltpu.make_async_copy(a, b, sems.at[len(backs)])
        back.start()
        backs.append(back)
    for back in backs:
        back.wait()


def last(*operands):
    _, piece_len, features = operands[0].shape
    shape = operands[1].shape
    small = (2, 1, piece_len, features)
    kv_heads = features // HD
    return pl.pallas_call(
        last_kernel,
        out_shape=(pltpu.HBM(shape, BF16),) * 2 + (pltpu.HBM(small, BF16),) * 2,
        in_specs=[in_vmem] * len(operands),
        out_specs=(in_hbm,) * 4,
        scratch_shapes=[pltpu.VMEM((piece_len, shape[3]), BF16)] * 4
        + [pltpu.VMEM(small, BF16)] * 2
        + [pltpu.SemaphoreType.DMA((4 + 2 * kv_heads,))],
        compiler_params=pltpu.CompilerParams(vmem_limit_bytes=VMEM_LIMIT),
        name="last",
    )(*operands)


def total_kernel(near_own, far_own, near_back, far_back, k_grad, v_grad, k_low, v_low, sems):
    near, far = near_slot(), far_slot()
    for n, low in enumerate((k_low, v_low)):
        low[near, 0] = (near_own[n] + near_back[n].astype(F32)).astype(BF16)
        low[far, 0] = (far_own[n] + far_back[n].astype(F32)).astype(BF16)
    for copy in fetch_pairs([(k_low, k_grad), (v_low, v_grad)], sems):
        copy.wait()


def total(*operands):
    _, piece_len, features = operands[0].shape
    shape = (2, 1, piece_len, features)
    return pl.pallas_call(
        total_kernel,
        out_shape=(pltpu.HBM(shape, BF16),) * 2,
        in_specs=[in_vmem] * len(operands),
        out_specs=(in_hbm,) * 2,
        scratch_shapes=[pltpu.VMEM(shape, BF16)] * 2 + [pltpu.SemaphoreType.DMA((2,))],
        compiler_params=pltpu.CompilerParams(vmem_limit_bytes=VMEM_LIMIT),
        name="total",
    )(*operands)


def far_links(pairs):
    low = [(i, i + 1, i) for i in range(3, pairs - 1, 2)]
    high = [(i + 1, i, 2 * pairs - 2 - i) for i in range(1, pairs - 3, 2)]
    return low + high


def hops(flow):
    (y, x, core), (to_y, to_x, to_core) = ((i // 4, i // 2 % 2, i % 2) for i in flow)
    steps = []
    if x != to_x:
        steps.append(("x", to_x, y))
    if y != to_y:
        steps.append(("y", to_y, to_x))
    return steps, core != to_core


def burden(flow, taken, late):
    steps, other_core = hops(flow)
    weight = 0.1
    if steps:
        weight = len(steps) + 0.3 * other_core + (1.5 if flow[1] == 0 else 0.5 * (flow[1] % 2))
        weight += 3.0 * sum(step in taken for step in steps)
        weight += 0.7 * (flow[1] in late)
    return weight


SPARE = {
    ((5, 6), (2, 1)): [(3, 2), (4, 5), (6, 7), (1, 0), (0, 3), (7, 4)],
    ((6, 5), (1, 2)): [(2, 3), (5, 4), (7, 6), (0, 1), (3, 0), (4, 7)],
}


def complete(route, pairs):
    if pairs == 8 and tuple(route) in SPARE:
        return route + SPARE[tuple(route)]
    sources = [i for i in range(pairs) if i not in {a for a, _ in route}]
    targets = [i for i in range(pairs) if i not in {b for _, b in route}]
    if pairs == 8:
        taken = {step for flow in route for step in hops(flow)[0]}
        late = {i for flow in route for i in flow}
        found = [(math.inf, [])]

        def search(rest_of, free, cost, chosen):
            if cost >= found[0][0]:
                return
            if not rest_of:
                found[0] = (cost, chosen)
                return
            for b in free:
                flow = (rest_of[0], b)
                if flow[0] != b:
                    left = [t for t in free if t != b]
                    more = burden(flow, taken, late)
                    search(rest_of[1:], left, cost + more, chosen + [flow])

        search(sources, targets, 0.0, [])
        if found[0][0] < math.inf:
            return route + found[0][1]
    for turn_by in range(len(targets)):
        turned = targets[turn_by:] + targets[:turn_by]
        if all(a != b for a, b in zip(sources, turned)):
            return route + list(zip(sources, turned))
    return route


def attend_pairs(links, queries, out_grad, doc, far_kv, near_kv):
    pairs = lax.axis_size("ctx")
    mates = [(i, i ^ 1) for i in range(pairs) if i ^ 1 < pairs]
    flows = [(a, b) for a, b, _ in links]
    far_kv, near_kv = keep(far_kv, near_kv)
    mate_kv = lax.ppermute(near_kv, "ctx", mates)
    if links:
        next_kv = lax.ppermute(far_kv, "ctx", complete(flows, pairs))
    weights, dprobs, stats = diagonal(doc, near_kv, queries, out_grad)
    mate_grads, far_own, p_far, ds_far = whole(stats, far_kv, mate_kv, queries, out_grad)
    mate_back = lax.ppermute(mate_grads, "ctx", mates)
    if not links:
        o_far, dq_far = far_side(far_kv, mate_kv, p_far, ds_far)
        return last(
            near_kv, queries, out_grad, weights, dprobs, stats, o_far, dq_far, far_own, mate_back
        )
    next_grads, p_next, ds_next, after = cross(
        doc, next_kv, queries, out_grad, stats, mate_grads
    )
    far_back = lax.ppermute(next_grads, "ctx", complete([(b, a) for a, b in flows], pairs))
    out, q_grad, near_own = rest(
        near_kv, queries, out_grad, weights, dprobs, after, far_kv, mate_kv, p_far, ds_far,
        next_kv, p_next, ds_next, shape=queries.shape,
    )
    k_grad, v_grad = total(near_own, far_own, mate_back, far_back)
    return (out, q_grad, k_grad, v_grad)


def local_pairs(queries, keys, values, out_grad, block_doc):
    links = far_links(lax.axis_size("ctx"))
    low = [link for link in links if link[0] < link[1]]
    high = [link for link in links if link[0] > link[1]]
    outer = [link for link in links if min(link[:2]) % 4 == 3]
    inner = [link for link in links if min(link[:2]) % 4 == 1]

    def needed(doc):
        def linked_among(*groups):
            some = [link for link in links if all(link in group for group in groups)]
            same = [doc[first] == doc[first + 1] for _, _, first in some]
            return functools.reduce(jnp.logical_or, same)

        any_outer = linked_among(outer)
        any_low, any_high = linked_among(low), linked_among(high)
        side = jnp.where(any_low, jnp.where(any_high, 4, 2), 3)
        near_only = jnp.where(linked_among(inner), 1, 0)
        return jnp.where(any_outer, side, near_only)

    far_kv, near_kv, case, doc = pick(keys, values, block_doc, needed)
    branches = [functools.partial(attend_pairs, some) for some in ([], inner, low, high, links)]
    return lax.switch(case[0], branches, queries, out_grad, doc, far_kv, near_kv)


def local(queries, keys, values, out_grad, block_doc):
    window = min(7, lax.axis_size("ctx") // 4 - 1) + 1
    piece_len = queries.shape[2]
    even = lax.axis_size("ctx") % 2 == 0
    if window == 2 and piece_len == BLOCK and even:
        return local_pairs(queries, keys, values, out_grad, block_doc)
    return local_wide(queries, keys, values, out_grad, block_doc)


def solution(mesh):
    in_specs = (
        P(None, "ctx", None, "tp"),
        P(None, "ctx", None, "tp"),
        P(None, "ctx", None, "tp"),
        P(None, "ctx", None, "tp"),
        P(),
    )
    out_specs = (
        P(None, "ctx", None, "tp"),
        P(None, "ctx", None, "tp"),
        P(None, "ctx", None, "tp"),
        P(None, "ctx", None, "tp"),
    )
    return jax.shard_map(local, mesh=mesh, in_specs=in_specs, out_specs=out_specs, check_vma=False)
```
